128 devices in a mesh: ctx: 16 (over x, z_hi, core), exp: 8 (over y, z_lo).
Axes of the slice: x: 4, y: 4, z: 4 (z_hi: 2, z_lo: 2; z = z_hi * 2 + z_lo), core: 2. Of those that a mesh axis runs over, the one named last changes fastest.
Arguments:
- queries: bfloat16 [128, 36864], P('ctx', 'exp'), may hold values from -82.5 to 82.5
- latents: bfloat16 [16384, 576], P('ctx'), may hold values from -4.5 to 4.5
- out_grad: bfloat16 [128, 32768], P('ctx', 'exp'), may hold values from -6 to 6
- hidden_rows: bfloat16 [16384, 5120], P(('ctx', 'exp')), may hold values from -6 to 6
- norm_gain: float32 [5120], replicated, may hold values from 0.25 to 4
- latent_proj: bfloat16 [5120, 576], replicated, may hold values from -0.078125 to 0.078125
- stream_grad: bfloat16 [16384, 5120], P(('ctx', 'exp')), may hold values from -6 to 6
- expert_ids: int32 [16384, 2], P(('ctx', 'exp')), may hold values from 0 to 7, all different within a row; in each aligned block of 128 rows (0 to 127, 128 to 255, ...) at most 64 rows name the same one
- route_weights: float32 [16384, 2], P(('ctx', 'exp')), may hold values from 0.1 to 1
- expert_acts: bfloat16 [8, 8192, 768], P('exp', 'ctx'), may hold values from -6 to 6
- down_proj: bfloat16 [8, 768, 5120], P('exp'), may hold values from -0.21875 to 0.21875
Outputs:
- query_grad: bfloat16 [128, 36864], P('ctx', 'exp')
- stream_total: bfloat16 [16384, 5120], P(('ctx', 'exp'))
- act_grad: bfloat16 [8, 8192, 768], P('exp', 'ctx')
- down_grad: bfloat16 [8, 768, 5120], P('exp', 'ctx')
- weight_grad: float32 [16384, 2], P(('ctx', 'exp'))
The draws below stay inside these ranges and needn't reach their ends.
Inputs may be any that keep to these rules, and one draw needn't show every extreme that they name: `expert_ids`: within the rows of one device no expert is named more than 64 times.
All inputs are finite; a program needn't handle non-finite values.
Results may differ from the reference program's by a relative error of at most 0.03.
Values may be sent and summed in bfloat16 or wider, within the bound.
A program may use at most 128 MiB of HBM per device.

```python
import math
import jax
import jax.numpy as jnp
import numpy as np
from jax import lax

D = 5120
HEADS = 64
LAT = 512
ROPE = 64
KEY = 576
FF = 768
TOP = 2
TOK_DEV = 1024
QROWS = 8
TOK_EXP = 128
CAP = 64
SLOTS = 512
EXPERTS = 8
TOKENS = 16384
N_CTX = 16
N_EXP = 8


def latent_base(key):
    return jnp.clip(jax.random.normal(jax.random.fold_in(key, 11), (TOKENS, KEY), jnp.float32), -4.5, 4.5)


def draw_latents(key, part):
    base = latent_base(key)
    return base.astype(jnp.bfloat16)


def draw_queries(key, part):
    key = jax.random.fold_in(key, 2)
    subkeys = jax.random.split(key, 1)
    query_count = N_CTX * QROWS
    noise = jnp.clip(jax.random.normal(subkeys[0], (query_count, HEADS * KEY), jnp.float32), -4.5, 4.5)
    return noise.astype(jnp.bfloat16)


def block_scale(key, extent, cuts, smallest, top_value):
    factor_of = 1.0
    for axis_at, parts in cuts:
        heights = jax.random.uniform(jax.random.fold_in(jax.random.fold_in(key, 6), axis_at), (parts,), jnp.float32, smallest / len(cuts), top_value / len(cuts))
        factor_of = factor_of * jnp.repeat(jnp.exp(heights), extent[axis_at] // parts).reshape((-1,) + (1,) * (len(extent) - 1 - axis_at))
    return factor_of


def shared_out(key, own, number, rows, count, top, reach, lean):
    sequence = jax.random.permutation(key, count)
    crowded, ordinary = portions_of(count, rows * top, reach, lean, True), portions_of(count, rows * top, reach, lean, False)
    places = jnp.arange(count)

    def named(sizes, offset_by):
        used = int((sizes > 0).sum())
        fixed = max(1, used // 4)
        moved = fixed + (places - fixed + offset_by * (used - fixed)) % max(1, count - fixed)
        return jnp.zeros((count,), jnp.int32).at[sequence[jnp.where(places < fixed, places, moved)]].set(jnp.asarray(sizes, jnp.int32))

    sizes = jnp.where(number % 4 == 0, named(crowded, number // 4), named(ordinary, number - number // 4 - 1))
    mixed = jax.random.permutation(jax.random.fold_in(own, 3), count)
    source_of, taker = mixed[0:count // 2 * 2:2], mixed[1:count // 2 * 2:2]
    margin = jnp.minimum(sizes[source_of] - 1, reach - sizes[taker]) // 2
    margin = jnp.where((source_of == sequence[0]) | (taker == sequence[0]) | (sizes[taker] == 0), 0, jnp.maximum(margin, 0))
    moved = jax.random.randint(jax.random.fold_in(own, 4), (count // 2,), 0, 1 << 20) % (margin + 1)
    sizes = sizes.at[source_of].add(-moved).at[taker].add(moved)
    items = jnp.searchsorted(jnp.cumsum(sizes), jnp.arange(rows * top), side="right").astype(jnp.int32)
    listing = items.reshape(top, rows).T
    listing = listing[jax.random.permutation(jax.random.fold_in(own, 1), rows)]
    offset_by = jax.random.randint(jax.random.fold_in(own, 2), (rows, 1), 0, top)
    return jnp.take_along_axis(listing, (jnp.arange(top)[None, :] + offset_by) % top, axis=1)


def portions_of(amount, total, bound, skew, full):
    weights = [(1 << 20) // math.isqrt(rank ** skew) + 1 for rank in range(1, amount + 1)]
    largest = bound if full else min(bound, max(-(-total // amount), total * weights[0] // sum(weights)))
    least = 1 if total - largest >= amount - 1 else 0
    given, rest = [largest] + [least] * (amount - 1), total - largest - least * (amount - 1)
    while rest > 0:
        candidates = [i for i in range(1, amount) if given[i] < largest] or [i for i in range(1, amount) if given[i] < bound]
        whole, remaining = sum([weights[i] for i in candidates]), rest
        for i in candidates:
            addition = min(bound - given[i], max(1, remaining * weights[i] // whole), rest)
            given[i] = given[i] + addition
            rest = rest - addition
    return np.array(given)


def scatter_about(own_key, shape, scale, most, cuts=(), kind=jnp.bfloat16):
    values = scale * jax.random.normal(own_key, shape, jnp.float32)
    if cuts:
        values = values * block_scale(own_key, shape, cuts, -0.22, 0.18)
    return jnp.clip(values, -most, most).astype(kind)


def setup_inputs(seed: int = 0) -> dict:
    arg_keys = jax.random.split(jax.random.key(seed), 12)
    queries = draw_queries(jax.random.fold_in(arg_keys[11], 71), 0)
    latents = draw_latents(jax.random.fold_in(arg_keys[11], 71), 0)
    out_grad = scatter_about(arg_keys[2], (N_CTX * QROWS, HEADS * LAT), 1.0, 6.0, ((0, 16), (1, 8)))
    hidden_rows = scatter_about(arg_keys[3], (TOKENS, D), 1.0, 6.0, ((0, 128),))
    norm_gain = jnp.clip(jnp.exp(jax.random.uniform(arg_keys[4], (D,), jnp.float32, math.log(0.25), math.log(4.0))), 0.25, 4.0)
    latent_proj = scatter_about(arg_keys[5], (D, KEY), D ** -0.5, 0.078125)
    stream_grad = scatter_about(arg_keys[6], (TOKENS, D), 0.5, 6.0, ((0, 128),))
    expert_ids_keys = jax.random.split(jax.random.fold_in(arg_keys[7], 1), TOKENS // TOK_EXP)
    expert_ids_turns = jax.random.permutation(jax.random.fold_in(arg_keys[7], 3), TOKENS // TOK_EXP)
    expert_ids = jax.vmap(lambda own, number: shared_out(jax.random.fold_in(arg_keys[7], 2), own, number, TOK_EXP, EXPERTS, TOP, CAP, 2))(expert_ids_keys, expert_ids_turns).reshape((TOKENS, TOP))
    route_weights = jnp.clip(0.1 + 0.9 * jax.random.uniform(arg_keys[8], (TOKENS, TOP), jnp.float32) ** block_scale(arg_keys[8], (TOKENS, TOP), ((0, 128),), -0.2, 0.2), 0.1, 1.0)
    expert_acts = scatter_about(arg_keys[9], (EXPERTS, N_CTX * SLOTS, FF), 1.0, 6.0, ((0, 8), (1, 16)))
    down_proj = scatter_about(arg_keys[10], (EXPERTS, FF, D), FF ** -0.5, 0.21875, ((0, 8),))
    return dict(queries=queries, latents=latents, out_grad=out_grad, hidden_rows=hidden_rows, norm_gain=norm_gain, latent_proj=latent_proj, stream_grad=stream_grad, expert_ids=expert_ids, route_weights=route_weights, expert_acts=expert_acts, down_proj=down_proj)


EPSILON = 1e-06
NEG_LARGE = -1e+30

def attention_grads(queries, latents, out_grad):
    score_scale = KEY ** (-0.5)
    query_count = N_CTX * QROWS
    row_index = jnp.arange(query_count, dtype=jnp.int32)
    query_pos = row_index // QROWS * TOK_DEV + TOK_DEV - QROWS + row_index % QROWS
    key_pos = jnp.arange(TOKENS, dtype=jnp.int32)
    visible = key_pos[None, :] <= query_pos[:, None]
    values = latents[:, :LAT]

    def one_head(key_total, head):
        query_cols = lax.dynamic_slice_in_dim(queries, head * KEY, KEY, 1)
        grad_cols = lax.dynamic_slice_in_dim(out_grad, head * LAT, LAT, 1)
        scores = jnp.dot(query_cols, latents.T, preferred_element_type=jnp.float32) * score_scale
        prob_grads = jnp.dot(grad_cols, values.T, preferred_element_type=jnp.float32)
        masked = jnp.where(visible, scores, NEG_LARGE)
        row_max = lax.optimization_barrier(jnp.max(masked, axis=1, keepdims=True))
        row_total = lax.optimization_barrier(jnp.sum(jnp.where(visible, jnp.exp(masked - row_max), 0.0), axis=1, keepdims=True))
        log_total = row_max + jnp.log(row_total)
        probs_now = jnp.where(visible, jnp.exp(masked - log_total), 0.0)
        row_delta = lax.optimization_barrier(jnp.sum(probs_now * prob_grads, axis=1, keepdims=True))
        score_grads = (probs_now * (prob_grads - row_delta)).astype(jnp.bfloat16)
        query_part = (jnp.dot(score_grads, latents, preferred_element_type=jnp.float32) * score_scale).astype(jnp.bfloat16)
        key_part = jnp.dot(score_grads.T, query_cols, preferred_element_type=jnp.float32) * score_scale
        value_part = jnp.dot(probs_now.astype(jnp.bfloat16).T, grad_cols, preferred_element_type=jnp.float32)
        key_part = key_part + jnp.pad(value_part, ((0, 0), (0, ROPE)))
        return (key_total + key_part, query_part)
    start_total = jnp.zeros((TOKENS, KEY), jnp.float32)
    key_total, head_grads = lax.scan(one_head, start_total, jnp.arange(HEADS, dtype=jnp.int32))
    query_grad = jnp.transpose(head_grads, (1, 0, 2)).reshape(query_count, HEADS * KEY)
    return (query_grad, key_total)

def slot_table(ids_row):
    chosen = (ids_row[:, None] == jnp.arange(N_EXP, dtype=jnp.int32)[None, :]).astype(jnp.int32)
    earlier = jnp.cumsum(chosen, axis=0) - chosen
    return ids_row * CAP + lax.optimization_barrier(jnp.sum(earlier * chosen, axis=1))

def reference(queries, latents, out_grad, hidden_rows, norm_gain, latent_proj, stream_grad, expert_ids, route_weights, expert_acts, down_proj):
    query_grad, key_total = attention_grads(queries, latents, out_grad)
    key_latent_grad = key_total.astype(jnp.bfloat16)
    norm_grad = jnp.dot(key_latent_grad, latent_proj.T, preferred_element_type=jnp.float32)
    row_values = hidden_rows.astype(jnp.float32)
    inverse = lax.rsqrt(lax.optimization_barrier(jnp.mean(row_values * row_values, axis=-1, keepdims=True)) + EPSILON)
    gained = norm_gain * norm_grad
    through_norm = inverse * gained - row_values * (inverse * inverse * inverse) * lax.optimization_barrier(jnp.mean(row_values * gained, axis=-1, keepdims=True))
    stream_total = (stream_grad.astype(jnp.float32) + through_norm).astype(jnp.bfloat16)
    flat_ids = expert_ids.reshape(N_CTX, N_EXP, TOK_EXP * TOP)
    slot_ids = jax.vmap(jax.vmap(slot_table))(flat_ids)
    select = (slot_ids[..., None] == jnp.arange(SLOTS, dtype=jnp.int32)).astype(jnp.float32)
    select = select.reshape(N_CTX, N_EXP, TOK_EXP, TOP, SLOTS)
    placing = lax.optimization_barrier(jnp.sum(select, axis=3))
    row_grads = stream_total.astype(jnp.float32).reshape(N_CTX, N_EXP, TOK_EXP, D)
    rounded_weights = lax.optimization_barrier(route_weights.astype(jnp.bfloat16)).astype(jnp.float32)
    rounded_weights = rounded_weights.reshape(N_CTX, N_EXP, TOK_EXP, TOP)
    weight_slots = jnp.einsum('abtks,abtk->abs', select, rounded_weights).astype(jnp.bfloat16)
    expert_rows = expert_acts.reshape(EXPERTS, N_CTX, SLOTS, FF)

    def one_expert(inputs):
        expert, acts_in, weight = inputs
        lower = expert * CAP
        place_now = lax.dynamic_slice_in_dim(placing, lower, CAP, 3)
        rows_in = jnp.einsum('abtr,abtd->abrd', place_now, row_grads).astype(jnp.bfloat16).reshape(N_CTX, SLOTS, D)
        weights_in = lax.dynamic_slice_in_dim(weight_slots, lower, CAP, 2).reshape(N_CTX, SLOTS)
        rows_wide = rows_in.astype(jnp.float32)
        scaled = (weights_in.astype(jnp.float32)[..., None] * rows_wide).astype(jnp.bfloat16)
        act_part = jnp.einsum('isd,fd->isf', scaled.astype(jnp.float32), weight.astype(jnp.float32)).astype(jnp.bfloat16)
        outputs = jnp.einsum('isf,fd->isd', acts_in.astype(jnp.float32), weight.astype(jnp.float32))
        slot_grads = lax.optimization_barrier(jnp.sum(rows_wide * outputs, axis=-1))
        terms = jnp.einsum('isf,isd->ifd', acts_in.astype(jnp.float32), scaled.astype(jnp.float32))
        terms = lax.optimization_barrier(terms.astype(jnp.bfloat16)).astype(jnp.float32)
        return (act_part, slot_grads, lax.optimization_barrier(jnp.sum(terms, axis=0)).astype(jnp.bfloat16))
    experts_list = jnp.arange(EXPERTS, dtype=jnp.int32)
    act_parts, slot_grads, down_grad = lax.map(one_expert, (experts_list, expert_rows, down_proj))
    returned = slot_grads.reshape(EXPERTS, N_CTX, N_EXP, CAP).transpose(1, 2, 0, 3).reshape(N_CTX, N_EXP, SLOTS)
    weight_grad = jnp.einsum('abtks,abs->abtk', select, returned).reshape(TOKENS, TOP)
    act_grad = act_parts.reshape(EXPERTS, N_CTX * SLOTS, FF)
    return (query_grad, stream_total, act_grad, down_grad, weight_grad)
```

```python
import functools
import jax
import jax.numpy as jnp
from jax import lax
from jax.experimental import pallas as pl
from jax.experimental.pallas import tpu as pltpu
from jax.sharding import PartitionSpec as P

EPSILON = 1e-06
NEG_LARGE = -1e30
MESH = pl.DeviceIdType.MESH
F32 = jnp.float32
BF16 = jnp.bfloat16
LANES = 128


def padded(width):
    return -(-width // LANES) * LANES


def nt_dot(a, b):
    return lax.dot_general(a, b, (((1,), (1,)), ((), ())), preferred_element_type=F32)


def tn_dot(a, b):
    return lax.dot_general(a, b, (((0,), (0,)), ((), ())), preferred_element_type=F32)


def push(src, dst, send, recv, where):
    return pltpu.make_async_remote_copy(
        src_ref=src, dst_ref=dst, send_sem=send, recv_sem=recv, device_id=where, device_id_type=MESH
    )


def greet(axes):
    barrier = pltpu.get_barrier_semaphore()
    total = 0
    for axis, count in axes:
        me = lax.axis_index(axis)

        @pl.loop(0, count)
        def _(i):
            @pl.when(i != me)
            def _():
                pl.semaphore_signal(barrier, inc=1, device_id={axis: i}, device_id_type=MESH)

        total += count - 1
    pl.semaphore_wait(barrier, total)


def attention_kernel(
    sizes,
    rows_ref,
    key_ref,
    key_out,
    query_out,
    rows_all,
    stats_all,
    keys,
    weights,
    grads,
    score_grads,
    key_parts,
    key_all,
    query_parts,
    query_all,
    rows_send,
    rows_recv,
    stats_send,
    stats_recv,
    key_send,
    key_recv,
    query_send,
    query_recv,
):
    n_ctx, n_exp, key_width, value_width, query_rows, heads = sizes
    wide = padded(key_width)
    me = lax.axis_index("ctx")
    mine = lax.axis_index("exp")
    key_count = key_ref.shape[0]
    per = query_rows * heads
    scale = key_width ** (-0.5)
    group = 4
    cols = group * per
    n_groups = n_ctx // group
    tiles = cols // LANES

    greet((("ctx", n_ctx), ("exp", n_exp)))

    def rows_copy(there, source):
        return push(
            rows_ref, rows_all.at[source], rows_send.at[there], rows_recv.at[source], {"ctx": there}
        )

    @pl.loop(0, me)
    def _(i):
        rows_copy(me - 1 - i, me).start()

    @pl.loop(0, me)
    def _(i):
        rows_all[i] = jnp.zeros(rows_all.shape[1:], BF16)

    rows_all[me] = rows_ref[...]
    keys[:, :key_width] = key_ref[...]
    keys[:, key_width:] = jnp.zeros((key_count, wide - key_width), BF16)

    @pl.loop(0, n_groups)
    def _(g):
        for k in range(group):
            b = g * group + k

            @pl.when(b > me)
            def _():
                rows_copy(0, b).wait_recv()

        block = rows_all[pl.ds(g * group, group)].reshape(cols, rows_all.shape[2])
        at = pl.ds(pl.multiple_of(g * cols, cols), cols)
        scores = nt_dot(keys[...], block[:, :wide]) * scale
        prob_grads = nt_dot(keys[:, :value_width], block[:, wide:])
        column = lax.broadcasted_iota(jnp.int32, (1, cols), 1)
        last = (
            (g * group + column // per - me) * key_count
            + key_count
            - query_rows
            + (column % per) // heads
        )
        visible = lax.broadcasted_iota(jnp.int32, (key_count, cols), 0) <= last
        masked = jnp.where(visible, scores, NEG_LARGE)
        top = jnp.max(masked, axis=0, keepdims=True)
        grown = jnp.where(visible, jnp.exp(masked - top), 0.0)
        total = jnp.sum(grown, axis=0, keepdims=True)
        dotted = jnp.sum(grown * prob_grads, axis=0, keepdims=True)
        weights[:, at] = grown
        grads[:, at] = prob_grads
        for k in range(tiles):
            part = slice(k * LANES, (k + 1) * LANES)
            for n, value in enumerate((top, total, dotted)):
                stats_all[me, n, pl.ds(g * tiles + k, 1)] = value[:, part]

    def stats_copy(there, source):
        return push(
            stats_all.at[source],
            stats_all.at[source],
            stats_send.at[there],
            stats_recv.at[source],
            {"ctx": there},
        )

    @pl.loop(0, n_ctx)
    def _(i):
        @pl.when(i != me)
        def _():
            stats_copy(i, me).start()

    @pl.loop(0, n_ctx)
    def _(i):
        @pl.when(i != me)
        def _():
            stats_copy(me, i).wait_recv()

    tops = stats_all[:, 0]
    peak = jnp.max(tops, axis=0)
    factors = jnp.exp(tops - peak[None])
    total = jnp.sum(stats_all[:, 1] * factors, axis=0)
    delta = jnp.sum(stats_all[:, 2] * factors, axis=0) / total
    share = jnp.exp(stats_all[me, 0] - peak) / total
    share_row = jnp.concatenate([share[n : n + 1] for n in range(share.shape[0])], axis=1)
    delta_row = jnp.concatenate([delta[n : n + 1] for n in range(delta.shape[0])], axis=1)

    def key_copy(there, source):
        return push(
            key_parts.at[there], key_all.at[source], key_send.at[there], key_recv.at[source], {"exp": there}
        )

    piece = key_count // n_exp
    step = 2 * piece

    @pl.loop(0, key_count // step)
    def _(n):
        at = pl.ds(pl.multiple_of(n * step, step), step)
        probs = weights[at, :] * share_row
        now = (probs * (grads[at, :] - delta_row)).astype(BF16)
        score_grads[at, :] = now
        flat = rows_all[...].reshape(n_ctx * per, rows_all.shape[2])
        through = jnp.dot(now, flat[:, :wide], preferred_element_type=F32) * scale
        value = jnp.dot(probs.astype(BF16), flat[:, wide:], preferred_element_type=F32)
        for k in range(2):
            part = slice(k * piece, (k + 1) * piece)
            key_parts[2 * n + k, :, :value_width] = (
                through[part, :value_width] + value[part]
            ).astype(BF16)
            key_parts[2 * n + k, :, value_width:] = through[part, value_width:].astype(BF16)

            @pl.when(2 * n + k != mine)
            def _():
                key_copy(2 * n + k, mine).start()

    key_all[mine] = key_parts[mine]

    def query_copy(there, source):
        return push(
            query_parts.at[there],
            query_all.at[source],
            query_send.at[there],
            query_recv.at[source],
            {"ctx": there},
        )

    @pl.loop(0, n_groups)
    def _(g):
        at = pl.ds(pl.multiple_of(g * cols, cols), cols)
        part = tn_dot(score_grads[:, at], keys[...]) * scale
        query_parts[pl.ds(g * group, group)] = part.astype(BF16).reshape(group, per, wide)
        for k in range(group):
            b = g * group + k

            @pl.when(b > me)
            def _():
                query_copy(b, me).start()

    @pl.loop(0, n_exp)
    def _(s):
        @pl.when(s != mine)
        def _():
            key_copy(mine, s).wait_recv()

    key_total = key_all[0].astype(F32)
    for s in range(1, n_exp):
        key_total = key_total + key_all[s].astype(F32)
    key_out[...] = key_total.astype(BF16)

    def add(i, so_far):
        query_copy(me, i).wait_recv()
        return so_far + query_all[i].astype(F32)

    query_out[...] = lax.fori_loop(0, me, add, query_parts[me].astype(F32)).astype(BF16)

    @pl.loop(0, me)
    def _(i):
        rows_copy(i, me).wait_send()

    @pl.loop(0, n_ctx)
    def _(i):
        @pl.when(i != me)
        def _():
            stats_copy(i, me).wait_send()

        @pl.when(i > me)
        def _():
            query_copy(i, me).wait_send()

    @pl.loop(0, n_exp)
    def _(s):
        @pl.when(s != mine)
        def _():
            key_copy(s, mine).wait_send()


def attention(queries, latents, out_grad):
    key_count, key_width = latents.shape
    query_rows = queries.shape[0]
    heads = queries.shape[1] // key_width
    value_width = out_grad.shape[1] // heads
    per = query_rows * heads
    wide = padded(key_width)
    n_ctx, n_exp = lax.axis_size("ctx"), lax.axis_size("exp")
    piece = key_count // n_exp
    total_rows = n_ctx * per
    rows = jnp.concatenate(
        [
            queries.reshape(per, key_width),
            jnp.zeros((per, wide - key_width), BF16),
            out_grad.reshape(per, value_width),
        ],
        axis=1,
    )
    sizes = (n_ctx, n_exp, key_width, value_width, query_rows, heads)
    vmem = pl.BlockSpec(memory_space=pltpu.VMEM)
    dma = pltpu.SemaphoreType.DMA
    key_rows, query_grad = pl.pallas_call(
        functools.partial(attention_kernel, sizes),
        out_shape=(
            jax.ShapeDtypeStruct((piece, wide), BF16),
            jax.ShapeDtypeStruct((per, wide), BF16),
        ),
        in_specs=[vmem, vmem],
        out_specs=(vmem, vmem),
        scratch_shapes=[
            pltpu.VMEM((n_ctx, per, wide + value_width), BF16),
            pltpu.VMEM((n_ctx, 3, total_rows // LANES, LANES), F32),
            pltpu.VMEM((key_count, wide), BF16),
            pltpu.VMEM((key_count, total_rows), F32),
            pltpu.VMEM((key_count, total_rows), F32),
            pltpu.VMEM((key_count, total_rows), BF16),
            pltpu.VMEM((n_exp, piece, wide), BF16),
            pltpu.VMEM((n_exp, piece, wide), BF16),
            pltpu.VMEM((n_ctx, per, wide), BF16),
            pltpu.VMEM((n_ctx, per, wide), BF16),
            dma((n_ctx,)),
            dma((n_ctx,)),
            dma((n_ctx,)),
            dma((n_ctx,)),
            dma((n_exp,)),
            dma((n_exp,)),
            dma((n_ctx,)),
            dma((n_ctx,)),
        ],
        compiler_params=pltpu.CompilerParams(
            collective_id=0, has_side_effects=True, vmem_limit_bytes=56 * 2**20
        ),
    )(rows, latents)
    query_grad = query_grad[:, :key_width].reshape(query_rows, heads * key_width)
    return query_grad, key_rows[:, :key_width]


def body(
    queries,
    latents,
    out_grad,
    hidden_rows,
    norm_gain,
    latent_proj,
    stream_grad,
    expert_ids,
    route_weights,
    expert_acts,
    down_proj,
):
    query_grad, key_rows = attention(queries, latents, out_grad)
    norm_grad = lax.dot_general(
        key_rows, latent_proj, (((1,), (1,)), ((), ())), preferred_element_type=jnp.float32
    )
    row_values = hidden_rows.astype(jnp.float32)
    inverse = lax.rsqrt(jnp.mean(row_values * row_values, axis=-1, keepdims=True) + EPSILON)
    gained = norm_gain * norm_grad
    through_norm = inverse * gained - row_values * (inverse * inverse * inverse) * jnp.mean(
        row_values * gained, axis=-1, keepdims=True
    )
    stream_total = (stream_grad.astype(jnp.float32) + through_norm).astype(jnp.bfloat16)
    expert_count = lax.axis_size("exp")
    slot_count = expert_acts.shape[1]
    capacity = slot_count // expert_count
    local_rows = expert_ids.shape[0]
    top_count = expert_ids.shape[1]
    flat_ids = expert_ids.reshape(-1)
    chosen = (flat_ids[:, None] == jnp.arange(expert_count, dtype=jnp.int32)[None, :]).astype(
        jnp.int32
    )
    earlier = jnp.cumsum(chosen, axis=0) - chosen
    slot_of = flat_ids * capacity + jnp.sum(earlier * chosen, axis=1)
    select = (slot_of[:, None] == jnp.arange(slot_count, dtype=jnp.int32)[None, :]).astype(
        jnp.float32
    )
    select = select.reshape(local_rows, top_count, slot_count)
    placing = jnp.sum(select, axis=1).astype(jnp.bfloat16)
    outgoing = lax.dot_general(
        placing, stream_total, (((0,), (0,)), ((), ())), preferred_element_type=jnp.float32
    ).astype(jnp.bfloat16)
    rounded_weights = lax.optimization_barrier(route_weights.astype(jnp.bfloat16)).astype(
        jnp.float32
    )
    weight_slots = jnp.einsum("tks,tk->s", select, rounded_weights).astype(jnp.bfloat16)
    arrived, arrived_weights = (
        lax.all_to_all(
            outgoing.reshape(expert_count, capacity, -1),
            "exp",
            split_axis=0,
            concat_axis=0,
            tiled=True,
        ),
        lax.all_to_all(
            weight_slots.reshape(expert_count, capacity),
            "exp",
            split_axis=0,
            concat_axis=0,
            tiled=True,
        ),
    )
    arrived = arrived.reshape(slot_count, -1)
    arrived_weights = arrived_weights.reshape(slot_count)
    expert_rows = expert_acts[0]
    weight = down_proj[0]
    scaled = (arrived_weights.astype(jnp.float32)[:, None] * arrived.astype(jnp.float32)).astype(
        jnp.bfloat16
    )
    act_grad = lax.dot_general(
        scaled, weight, (((1,), (1,)), ((), ())), preferred_element_type=jnp.float32
    ).astype(jnp.bfloat16)
    outputs = jnp.dot(expert_rows, weight, preferred_element_type=jnp.float32)
    slot_grads = jnp.sum(arrived.astype(jnp.float32) * outputs, axis=1)
    returned = lax.all_to_all(
        slot_grads.reshape(expert_count, capacity), "exp", split_axis=0, concat_axis=0, tiled=True
    ).reshape(slot_count)
    weight_grad = jnp.einsum("tks,s->tk", select, returned)
    down_share = lax.psum_scatter(
        lax.dot_general(
            expert_rows, scaled, (((0,), (0,)), ((), ())), preferred_element_type=jnp.float32
        ).astype(jnp.bfloat16),
        "ctx",
        scatter_dimension=0,
        tiled=True,
    )
    return (query_grad, stream_total, act_grad[None], down_share[None], weight_grad)


def solution(mesh):
    in_specs = (
        P("ctx", "exp"),
        P("ctx", None),
        P("ctx", "exp"),
        P(("ctx", "exp"), None),
        P(),
        P(),
        P(("ctx", "exp"), None),
        P(("ctx", "exp"), None),
        P(("ctx", "exp"), None),
        P("exp", "ctx", None),
        P("exp", None, None),
    )
    out_specs = (
        P("ctx", "exp"),
        P(("ctx", "exp"), None),
        P("exp", "ctx", None),
        P("exp", "ctx", None),
        P(("ctx", "exp"), None),
    )
    return jax.shard_map(body, mesh=mesh, in_specs=in_specs, out_specs=out_specs, check_vma=False)
```

```python
import functools
import jax
import jax.numpy as jnp
from jax import lax
from jax.experimental import pallas as pl
from jax.experimental.pallas import tpu as pltpu
from jax.sharding import PartitionSpec as P

EPSILON = 1e-06
NEG_LARGE = -1e30
MESH = pl.DeviceIdType.MESH
F32 = jnp.float32
BF16 = jnp.bfloat16
LANES = 128


def padded(width):
    return -(-width // LANES) * LANES


def nt_dot(a, b):
    return lax.dot_general(a, b, (((1,), (1,)), ((), ())), preferred_element_type=F32)


def tn_dot(a, b):
    return lax.dot_general(a, b, (((0,), (0,)), ((), ())), preferred_element_type=F32)


def push(src, dst, send, recv, where):
    return pltpu.make_async_remote_copy(
        src_ref=src, dst_ref=dst, send_sem=send, recv_sem=recv, device_id=where, device_id_type=MESH
    )


def greet(axes):
    barrier = pltpu.get_barrier_semaphore()
    total = 0
    for axis, count in axes:
        me = lax.axis_index(axis)

        @pl.loop(0, count)
        def _(i):
            @pl.when(i != me)
            def _():
                pl.semaphore_signal(barrier, inc=1, device_id={axis: i}, device_id_type=MESH)

        total += count - 1
    pl.semaphore_wait(barrier, total)


def attention_kernel(
    sizes,
    rows_ref,
    key_ref,
    key_out,
    query_out,
    rows_all,
    stats_all,
    keys,
    weights,
    grads,
    score_grads,
    key_parts,
    key_all,
    query_parts,
    query_all,
    rows_send,
    rows_recv,
    stats_send,
    stats_recv,
    key_send,
    key_recv,
    query_send,
    query_recv,
):
    n_ctx, n_exp, key_width, value_width, query_rows, heads = sizes
    wide = padded(key_width)
    me = lax.axis_index("ctx")
    mine = lax.axis_index("exp")
    key_count = key_ref.shape[0]
    per = query_rows * heads
    scale = key_width ** (-0.5)
    group = 4
    cols = group * per
    n_groups = n_ctx // group
    tiles = cols // LANES

    greet((("ctx", n_ctx), ("exp", n_exp)))

    def rows_copy(there, source):
        return push(
            rows_ref, rows_all.at[source], rows_send.at[there], rows_recv.at[source], {"ctx": there}
        )

    @pl.loop(0, me)
    def _(i):
        rows_copy(me - 1 - i, me).start()

    @pl.loop(0, me)
    def _(i):
        rows_all[i] = jnp.zeros(rows_all.shape[1:], BF16)

    rows_all[me] = rows_ref[...]
    keys[:, :key_width] = key_ref[...]
    keys[:, key_width:] = jnp.zeros((key_count, wide - key_width), BF16)

    @pl.loop(0, n_groups)
    def _(g):
        for k in range(group):
            b = g * group + k

            @pl.when(b > me)
            def _():
                rows_copy(0, b).wait_recv()

        block = rows_all[pl.ds(g * group, group)].reshape(cols, rows_all.shape[2])
        at = pl.ds(pl.multiple_of(g * cols, cols), cols)
        scores = nt_dot(keys[...], block[:, :wide]) * scale
        prob_grads = nt_dot(keys[:, :value_width], block[:, wide:])
        column = lax.broadcasted_iota(jnp.int32, (1, cols), 1)
        last = (
            (g * group + column // per - me) * key_count
            + key_count
            - query_rows
            + (column % per) // heads
        )
        visible = lax.broadcasted_iota(jnp.int32, (key_count, cols), 0) <= last
        masked = jnp.where(visible, scores, NEG_LARGE)
        top = jnp.max(masked, axis=0, keepdims=True)
        grown = jnp.where(visible, jnp.exp(masked - top), 0.0)
        total = jnp.sum(grown, axis=0, keepdims=True)
        dotted = jnp.sum(grown * prob_grads, axis=0, keepdims=True)
        weights[:, at] = grown
        grads[:, at] = prob_grads
        for k in range(tiles):
            part = slice(k * LANES, (k + 1) * LANES)
            for n, value in enumerate((top, total, dotted)):
                stats_all[me, n, pl.ds(g * tiles + k, 1)] = value[:, part]

    def stats_copy(there, source):
        return push(
            stats_all.at[source],
            stats_all.at[source],
            stats_send.at[there],
            stats_recv.at[source],
            {"ctx": there},
        )

    @pl.loop(0, n_ctx)
    def _(i):
        @pl.when(i != me)
        def _():
            stats_copy(i, me).start()

    @pl.loop(0, n_ctx)
    def _(i):
        @pl.when(i != me)
        def _():
            stats_copy(me, i).wait_recv()

    tops = stats_all[:, 0]
    peak = jnp.max(tops, axis=0)
    factors = jnp.exp(tops - peak[None])
    total = jnp.sum(stats_all[:, 1] * factors, axis=0)
    delta = jnp.sum(stats_all[:, 2] * factors, axis=0) / total
    share = jnp.exp(stats_all[me, 0] - peak) / total
    share_row = jnp.concatenate([share[n : n + 1] for n in range(share.shape[0])], axis=1)
    delta_row = jnp.concatenate([delta[n : n + 1] for n in range(delta.shape[0])], axis=1)

    def key_copy(there, source):
        return push(
            key_parts.at[there], key_all.at[source], key_send.at[there], key_recv.at[source], {"exp": there}
        )

    piece = key_count // n_exp
    step = 2 * piece

    @pl.loop(0, key_count // step)
    def _(n):
        at = pl.ds(pl.multiple_of(n * step, step), step)
        probs = weights[at, :] * share_row
        now = (probs * (grads[at, :] - delta_row)).astype(BF16)
        score_grads[at, :] = now
        flat = rows_all[...].reshape(n_ctx * per, rows_all.shape[2])
        through = jnp.dot(now, flat[:, :wide], preferred_element_type=F32) * scale
        value = jnp.dot(probs.astype(BF16), flat[:, wide:], preferred_element_type=F32)
        for k in range(2):
            part = slice(k * piece, (k + 1) * piece)
            key_parts[2 * n + k, :, :value_width] = (
                through[part, :value_width] + value[part]
            ).astype(BF16)
            key_parts[2 * n + k, :, value_width:] = through[part, value_width:].astype(BF16)

            @pl.when(2 * n + k != mine)
            def _():
                key_copy(2 * n + k, mine).start()

    key_all[mine] = key_parts[mine]

    def query_copy(there, source):
        return push(
            query_parts.at[there],
            query_all.at[source],
            query_send.at[there],
            query_recv.at[source],
            {"ctx": there},
        )

    @pl.loop(0, n_groups)
    def _(g):
        at = pl.ds(pl.multiple_of(g * cols, cols), cols)
        part = tn_dot(score_grads[:, at], keys[...]) * scale
        query_parts[pl.ds(g * group, group)] = part.astype(BF16).reshape(group, per, wide)
        for k in range(group):
            b = g * group + k

            @pl.when(b > me)
            def _():
                query_copy(b, me).start()

    @pl.loop(0, n_exp)
    def _(s):
        @pl.when(s != mine)
        def _():
            key_copy(mine, s).wait_recv()

    key_total = key_all[0].astype(F32)
    for s in range(1, n_exp):
        key_total = key_total + key_all[s].astype(F32)
    key_out[...] = key_total.astype(BF16)

    def add(i, so_far):
        query_copy(me, i).wait_recv()
        return so_far + query_all[i].astype(F32)

    query_out[...] = lax.fori_loop(0, me, add, query_parts[me].astype(F32)).astype(BF16)

    @pl.loop(0, me)
    def _(i):
        rows_copy(i, me).wait_send()

    @pl.loop(0, n_ctx)
    def _(i):
        @pl.when(i != me)
        def _():
            stats_copy(i, me).wait_send()

        @pl.when(i > me)
        def _():
            query_copy(i, me).wait_send()

    @pl.loop(0, n_exp)
    def _(s):
        @pl.when(s != mine)
        def _():
            key_copy(s, mine).wait_send()


def attention(queries, latents, out_grad):
    key_count, key_width = latents.shape
    query_rows = queries.shape[0]
    heads = queries.shape[1] // key_width
    value_width = out_grad.shape[1] // heads
    per = query_rows * heads
    wide = padded(key_width)
    n_ctx, n_exp = lax.axis_size("ctx"), lax.axis_size("exp")
    piece = key_count // n_exp
    total_rows = n_ctx * per
    rows = jnp.concatenate(
        [
            queries.reshape(per, key_width),
            jnp.zeros((per, wide - key_width), BF16),
            out_grad.reshape(per, value_width),
        ],
        axis=1,
    )
    sizes = (n_ctx, n_exp, key_width, value_width, query_rows, heads)
    vmem = pl.BlockSpec(memory_space=pltpu.VMEM)
    dma = pltpu.SemaphoreType.DMA
    key_rows, query_grad = pl.pallas_call(
        functools.partial(attention_kernel, sizes),
        out_shape=(
            jax.ShapeDtypeStruct((piece, wide), BF16),
            jax.ShapeDtypeStruct((per, wide), BF16),
        ),
        in_specs=[vmem, vmem],
        out_specs=(vmem, vmem),
        scratch_shapes=[
            pltpu.VMEM((n_ctx, per, wide + value_width), BF16),
            pltpu.VMEM((n_ctx, 3, total_rows // LANES, LANES), F32),
            pltpu.VMEM((key_count, wide), BF16),
            pltpu.VMEM((key_count, total_rows), F32),
            pltpu.VMEM((key_count, total_rows), F32),
            pltpu.VMEM((key_count, total_rows), BF16),
            pltpu.VMEM((n_exp, piece, wide), BF16),
            pltpu.VMEM((n_exp, piece, wide), BF16),
            pltpu.VMEM((n_ctx, per, wide), BF16),
            pltpu.VMEM((n_ctx, per, wide), BF16),
            dma((n_ctx,)),
            dma((n_ctx,)),
            dma((n_ctx,)),
            dma((n_ctx,)),
            dma((n_exp,)),
            dma((n_exp,)),
            dma((n_ctx,)),
            dma((n_ctx,)),
        ],
        compiler_params=pltpu.CompilerParams(
            collective_id=0, has_side_effects=True, vmem_limit_bytes=56 * 2**20
        ),
    )(rows, latents)
    query_grad = query_grad[:, :key_width].reshape(query_rows, heads * key_width)
    return query_grad, key_rows[:, :key_width]


def expert_kernel(
    sizes,
    stream_ref,
    placing_ref,
    slot_weights_ref,
    acts_ref,
    proj_hbm,
    act_out,
    down_out,
    returned,
    proj,
    outgoing,
    arrived,
    weights_in,
    acts_t,
    through,
    partial,
    core_in,
    x_in,
    z_part,
    z_in,
    slot_parts,
    proj_sem,
    slot_send,
    slot_recv,
    weight_send,
    weight_recv,
    core_send,
    core_recv,
    x_send,
    x_recv,
    z_send,
    z_recv,
    back_send,
    back_recv,
):
    n_ctx, n_exp, chunks, n_x, n_z = sizes
    me = lax.axis_index("ctx")
    mine = lax.axis_index("exp")
    core = lax.rem(me, 2)
    z_at = lax.rem(me // 2, n_z)
    x_at = me // (2 * n_z)
    depth = stream_ref.shape[1] // chunks
    slots, inner = acts_ref.shape
    capacity = slots // n_exp
    chips = n_ctx // 2
    share = inner // n_ctx

    def columns(c):
        return pl.ds(pl.multiple_of(c * depth, depth), depth)

    def proj_copy(c):
        return pltpu.make_async_copy(proj_hbm.at[:, columns(c)], proj.at[c], proj_sem.at[c])

    @pl.loop(0, chunks)
    def _(c):
        proj_copy(c).start()

    greet((("ctx", n_ctx), ("exp", n_exp)))

    def weight_copy(there, source):
        return push(
            slot_weights_ref.at[there],
            weights_in.at[source],
            weight_send.at[there],
            weight_recv.at[source],
            {"exp": there},
        )

    def slot_copy(c, there, source):
        return push(
            outgoing.at[c, there],
            arrived.at[c, source],
            slot_send.at[c, there],
            slot_recv.at[c, source],
            {"exp": there},
        )

    def core_copy(c):
        return push(
            partial.at[c, 1 - core], core_in.at[c], core_send.at[c], core_recv.at[c], {"ctx": me + 1 - 2 * core}
        )

    def x_copy(c, there, source):
        return push(
            partial.at[c, core, there],
            x_in.at[c, source],
            x_send.at[c, there],
            x_recv.at[c, source],
            {"ctx": (there * n_z + z_at) * 2 + core},
        )

    def z_copy(c):
        return push(
            z_part.at[c, 1 - z_at],
            z_in.at[c],
            z_send.at[c],
            z_recv.at[c],
            {"ctx": (x_at * n_z + 1 - z_at) * 2 + core},
        )

    def back_copy(there, source):
        return push(
            slot_parts.at[there], returned.at[source], back_send.at[there], back_recv.at[source], {"exp": there}
        )

    @pl.loop(1, n_exp)
    def _(k):
        weight_copy(lax.rem(mine + k, n_exp), mine).start()

    weights_in[mine] = slot_weights_ref[mine]

    @pl.loop(0, chunks)
    def _(c):
        placed = jnp.dot(placing_ref[...], stream_ref[:, columns(c)], preferred_element_type=F32)
        outgoing[c] = placed.astype(BF16).reshape(n_exp, capacity, depth)

        @pl.loop(1, n_exp)
        def _(k):
            slot_copy(c, lax.rem(mine + k, n_exp), mine).start()

        arrived[c, mine] = outgoing[c, mine]

    @pl.loop(1, n_exp)
    def _(k):
        weight_copy(mine, lax.rem(mine + k, n_exp)).wait_recv()

    slot_weight = weights_in[...].reshape(slots, LANES).astype(F32)[:, :1]
    turned = (acts_ref[...].astype(F32) * slot_weight).T.astype(BF16)
    for q in range(chips):
        for s in range(2):
            at = (q * 2 + s) * share
            to = (s * chips + q) * share
            acts_t[to : to + share] = turned[at : at + share]

    through[...] = jnp.zeros(through.shape, F32)

    @pl.loop(0, chunks + 3)
    def _(c):
        @pl.when(c < chunks)
        def _():
            @pl.loop(1, n_exp)
            def _(k):
                slot_copy(c, mine, lax.rem(mine + k, n_exp)).wait_recv()

            proj_copy(c).wait()
            rows = arrived[c].reshape(slots, depth)
            down = jnp.dot(acts_t[...], rows, preferred_element_type=F32)
            partial[c] = down.astype(BF16).reshape(2, n_x, n_z, share, depth)
            core_copy(c).start()
            through[...] += nt_dot(rows, proj[c])

        @pl.when((c >= 1) & (c < chunks + 1))
        def _():
            d = c - 1
            core_copy(d).wait_recv()
            total = partial[d, core].astype(F32) + core_in[d].astype(F32)
            partial[d, core] = total.astype(BF16)
            x_in[d, x_at] = partial[d, core, x_at]

            @pl.loop(1, n_x)
            def _(k):
                x_copy(d, lax.rem(x_at + k, n_x), x_at).start()

        @pl.when((c >= 2) & (c < chunks + 2))
        def _():
            d = c - 2

            @pl.loop(1, n_x)
            def _(k):
                x_copy(d, x_at, lax.rem(x_at + k, n_x)).wait_recv()

            total = x_in[d, 0].astype(F32)
            for k in range(1, n_x):
                total = total + x_in[d, k].astype(F32)
            z_part[d] = total.astype(BF16)
            z_copy(d).start()

        @pl.when(c >= 3)
        def _():
            d = c - 3
            z_copy(d).wait_recv()
            total = z_part[d, z_at].astype(F32) + z_in[d].astype(F32)
            down_out[:, columns(d)] = total.astype(BF16)

        @pl.when(c == chunks - 1)
        def _():
            all_through = through[...]
            act_out[...] = (all_through * slot_weight).astype(BF16)
            sums = jnp.sum(acts_ref[...].astype(F32) * all_through, axis=1, keepdims=True)
            slot_parts[...] = jnp.broadcast_to(sums, (slots, LANES)).reshape(slot_parts.shape)

            @pl.loop(1, n_exp)
            def _(k):
                back_copy(lax.rem(mine + k, n_exp), mine).start()

            returned[mine] = slot_parts[mine]

    @pl.loop(1, n_exp)
    def _(k):
        there = lax.rem(mine + k, n_exp)
        back_copy(mine, there).wait_recv()
        back_copy(there, mine).wait_send()
        weight_copy(there, mine).wait_send()

    @pl.loop(0, chunks)
    def _(c):
        @pl.loop(1, n_exp)
        def _(k):
            slot_copy(c, lax.rem(mine + k, n_exp), mine).wait_send()

        core_copy(c).wait_send()

        @pl.loop(1, n_x)
        def _(k):
            x_copy(c, lax.rem(x_at + k, n_x), x_at).wait_send()

        z_copy(c).wait_send()


def experts(stream_total, placing, slot_weights, acts, proj):
    n_ctx, n_exp = lax.axis_size("ctx"), lax.axis_size("exp")
    slots, inner = acts.shape
    width = stream_total.shape[1]
    capacity = slots // n_exp
    chunks = 10
    n_z = 2
    n_x = n_ctx // (2 * n_z)
    depth = width // chunks
    share = inner // n_ctx
    chips = n_ctx // 2
    wide_weights = jnp.broadcast_to(slot_weights[:, None], (slots, LANES)).reshape(n_exp, capacity, LANES)
    vmem = pl.BlockSpec(memory_space=pltpu.VMEM)
    dma = pltpu.SemaphoreType.DMA
    return pl.pallas_call(
        functools.partial(expert_kernel, (n_ctx, n_exp, chunks, n_x, n_z)),
        out_shape=(
            jax.ShapeDtypeStruct((slots, inner), BF16),
            jax.ShapeDtypeStruct((share, width), BF16),
            jax.ShapeDtypeStruct((n_exp, capacity, LANES), F32),
        ),
        in_specs=[vmem, vmem, vmem, vmem, pl.BlockSpec(memory_space=pl.ANY)],
        out_specs=(vmem, vmem, vmem),
        scratch_shapes=[
            pltpu.VMEM((chunks, inner, depth), BF16),
            pltpu.VMEM((chunks, n_exp, capacity, depth), BF16),
            pltpu.VMEM((chunks, n_exp, capacity, depth), BF16),
            pltpu.VMEM((n_exp, capacity, LANES), BF16),
            pltpu.VMEM((inner, slots), BF16),
            pltpu.VMEM((slots, inner), F32),
            pltpu.VMEM((chunks, 2, n_x, n_z, share, depth), BF16),
            pltpu.VMEM((chunks, n_x, n_z, share, depth), BF16),
            pltpu.VMEM((chunks, n_x, n_z, share, depth), BF16),
            pltpu.VMEM((chunks, n_z, share, depth), BF16),
            pltpu.VMEM((chunks, share, depth), BF16),
            pltpu.VMEM((n_exp, capacity, LANES), F32),
            dma((chunks,)),
            dma((chunks, n_exp)),
            dma((chunks, n_exp)),
            dma((n_exp,)),
            dma((n_exp,)),
            dma((chunks,)),
            dma((chunks,)),
            dma((chunks, n_x)),
            dma((chunks, n_x)),
            dma((chunks,)),
            dma((chunks,)),
            dma((n_exp,)),
            dma((n_exp,)),
        ],
        compiler_params=pltpu.CompilerParams(
            collective_id=1, has_side_effects=True, vmem_limit_bytes=60 * 2**20
        ),
    )(stream_total, placing, wide_weights, acts, proj)


def body(
    queries,
    latents,
    out_grad,
    hidden_rows,
    norm_gain,
    latent_proj,
    stream_grad,
    expert_ids,
    route_weights,
    expert_acts,
    down_proj,
):
    query_grad, key_rows = attention(queries, latents, out_grad)
    norm_grad = lax.dot_general(
        key_rows, latent_proj, (((1,), (1,)), ((), ())), preferred_element_type=jnp.float32
    )
    row_values = hidden_rows.astype(jnp.float32)
    inverse = lax.rsqrt(jnp.mean(row_values * row_values, axis=-1, keepdims=True) + EPSILON)
    gained = norm_gain * norm_grad
    through_norm = inverse * gained - row_values * (inverse * inverse * inverse) * jnp.mean(
        row_values * gained, axis=-1, keepdims=True
    )
    stream_total = (stream_grad.astype(jnp.float32) + through_norm).astype(jnp.bfloat16)
    expert_count = lax.axis_size("exp")
    slot_count = expert_acts.shape[1]
    capacity = slot_count // expert_count
    local_rows = expert_ids.shape[0]
    top_count = expert_ids.shape[1]
    flat_ids = expert_ids.reshape(-1)
    chosen = (flat_ids[:, None] == jnp.arange(expert_count, dtype=jnp.int32)[None, :]).astype(
        jnp.int32
    )
    earlier = jnp.cumsum(chosen, axis=0) - chosen
    slot_of = flat_ids * capacity + jnp.sum(earlier * chosen, axis=1)
    select = (slot_of[:, None] == jnp.arange(slot_count, dtype=jnp.int32)[None, :]).astype(
        jnp.float32
    )
    select = select.reshape(local_rows, top_count, slot_count)
    placing = jnp.sum(select, axis=1).astype(jnp.bfloat16)
    rounded_weights = lax.optimization_barrier(route_weights.astype(jnp.bfloat16)).astype(
        jnp.float32
    )
    weight_slots = jnp.einsum("tks,tk->s", select, rounded_weights).astype(jnp.bfloat16)
    act_grad, down_share, returned = experts(
        stream_total, placing.T, weight_slots, expert_acts[0], down_proj[0]
    )
    weight_grad = jnp.einsum("tks,s->tk", select, returned[:, :, 0].reshape(slot_count))
    return (query_grad, stream_total, act_grad[None], down_share[None], weight_grad)


def solution(mesh):
    in_specs = (
        P("ctx", "exp"),
        P("ctx", None),
        P("ctx", "exp"),
        P(("ctx", "exp"), None),
        P(),
        P(),
        P(("ctx", "exp"), None),
        P(("ctx", "exp"), None),
        P(("ctx", "exp"), None),
        P("exp", "ctx", None),
        P("exp", None, None),
    )
    out_specs = (
        P("ctx", "exp"),
        P(("ctx", "exp"), None),
        P("exp", "ctx", None),
        P("exp", "ctx", None),
        P(("ctx", "exp"), None),
    )
    return jax.shard_map(body, mesh=mesh, in_specs=in_specs, out_specs=out_specs, check_vma=False)
```

```python
import functools
import jax
import jax.numpy as jnp
from jax import lax
from jax.experimental import pallas as pl
from jax.experimental.pallas import tpu as pltpu
from jax.sharding import PartitionSpec as P

EPSILON = 1e-06
NEG_LARGE = -1e30
MESH = pl.DeviceIdType.MESH
F32 = jnp.float32
BF16 = jnp.bfloat16
LANES = 128


def padded(width):
    return -(-width // LANES) * LANES


def nt_dot(a, b):
    return lax.dot_general(a, b, (((1,), (1,)), ((), ())), preferred_element_type=F32)


def tn_dot(a, b):
    return lax.dot_general(a, b, (((0,), (0,)), ((), ())), preferred_element_type=F32)


def push(src, dst, send, recv, where):
    return pltpu.make_async_remote_copy(
        src_ref=src, dst_ref=dst, send_sem=send, recv_sem=recv, device_id=where, device_id_type=MESH
    )


def greet(axes):
    barrier = pltpu.get_barrier_semaphore()
    total = 0
    for axis, count in axes:
        me = lax.axis_index(axis)

        @pl.loop(0, count)
        def _(i):
            @pl.when(i != me)
            def _():
                pl.semaphore_signal(barrier, inc=1, device_id={axis: i}, device_id_type=MESH)

        total += count - 1
    pl.semaphore_wait(barrier, total)


def meet(peers):
    barrier = pltpu.get_barrier_semaphore()
    for where in peers:
        pl.semaphore_signal(barrier, inc=1, device_id=where, device_id_type=MESH)
    pl.semaphore_wait(barrier, len(peers))


def attention_kernel(
    sizes,
    queries_ref,
    out_grad_ref,
    latents_t_ref,
    gain_ref,
    hidden_hbm,
    stream_hbm,
    proj_t_hbm,
    stream_out,
    query_out,
    rows_all,
    stats_all,
    keys,
    weights,
    grads,
    score_grads,
    key_parts,
    key_all,
    hidden,
    stream,
    proj_t,
    load_sem,
    rows_send,
    rows_recv,
    pass_send,
    stats_send,
    stats_recv,
    key_send,
    key_recv,
):
    n_ctx, n_exp, key_width, value_width, query_rows, heads = sizes
    wide = padded(key_width)
    me = lax.axis_index("ctx")
    mine = lax.axis_index("exp")
    core = lax.rem(me, 2)
    sibling = me + 1 - 2 * core
    key_count = latents_t_ref.shape[1]
    width = gain_ref.shape[1]
    per = query_rows * heads
    scale = key_width ** (-0.5)
    group = 4
    cols = group * per
    n_groups = n_ctx // group
    tiles = cols // LANES
    first = me // group

    hidden_load = pltpu.make_async_copy(hidden_hbm, hidden, load_sem.at[0])
    proj_load = pltpu.make_async_copy(proj_t_hbm, proj_t.at[:key_width], load_sem.at[1])
    stream_load = pltpu.make_async_copy(stream_hbm, stream, load_sem.at[2])
    for copy in (hidden_load, proj_load, stream_load):
        copy.start()

    query_values = queries_ref[...].astype(F32)
    grad_values = out_grad_ref[...].astype(F32)
    rows_all[me, :, :key_width] = jnp.concatenate(
        [query_values[:, h * key_width : (h + 1) * key_width] for h in range(heads)], axis=0
    ).astype(BF16)
    rows_all[me, :, key_width:wide] = jnp.zeros((per, wide - key_width), BF16)
    rows_all[me, :, wide:] = jnp.concatenate(
        [grad_values[:, h * value_width : (h + 1) * value_width] for h in range(heads)], axis=0
    ).astype(BF16)

    greet((("ctx", n_ctx), ("exp", n_exp)))

    def rows_copy(there, source):
        return push(
            rows_all.at[source],
            rows_all.at[source],
            rows_send.at[there],
            rows_recv.at[source],
            {"ctx": there},
        )

    def pass_copy(source):
        return push(
            rows_all.at[source],
            rows_all.at[source],
            pass_send.at[source],
            rows_recv.at[source],
            {"ctx": sibling},
        )

    @pl.loop(0, me // 2)
    def _(i):
        rows_copy(me - 2 - 2 * i, me).start()

    @pl.when(core == 1)
    def _():
        pass_copy(me).start()

    @pl.loop(0, me)
    def _(i):
        rows_all[i] = jnp.zeros(rows_all.shape[1:], BF16)

    keys[:, :key_width] = latents_t_ref[...].T
    keys[:, key_width:] = jnp.zeros((key_count, wide - key_width), BF16)
    proj_t[key_width:] = jnp.zeros((wide - key_width, width), BF16)
    stats_all[me, 0] = jnp.full(stats_all.shape[2:], NEG_LARGE, F32)
    stats_all[me, 1] = jnp.zeros(stats_all.shape[2:], F32)
    stats_all[me, 2] = jnp.zeros(stats_all.shape[2:], F32)

    @pl.loop(0, first)
    def _(g):
        at = pl.ds(pl.multiple_of(g * cols, cols), cols)
        weights[:, at] = jnp.zeros((key_count, cols), F32)
        grads[:, at] = jnp.zeros((key_count, cols), F32)

    def compute(g):
        for k in range(n_groups // 2):
            b = g * group + 2 * k + 1 - core

            @pl.when(b > me)
            def _():
                pass_copy(b).wait_recv()

        block = rows_all[pl.ds(g * group, group)].reshape(cols, rows_all.shape[2])
        at = pl.ds(pl.multiple_of(g * cols, cols), cols)
        scores = nt_dot(keys[...], block[:, :wide]) * scale
        prob_grads = nt_dot(keys[:, :value_width], block[:, wide:])
        column = lax.broadcasted_iota(jnp.int32, (1, cols), 1)
        last = (
            (g * group + column // per - me) * key_count
            + key_count
            - query_rows
            + column % query_rows
        )
        visible = lax.broadcasted_iota(jnp.int32, (key_count, cols), 0) <= last
        masked = jnp.where(visible, scores, NEG_LARGE)
        top = jnp.max(masked, axis=0, keepdims=True)
        grown = jnp.where(visible, jnp.exp(masked - top), 0.0)
        total = jnp.sum(grown, axis=0, keepdims=True)
        dotted = jnp.sum(grown * prob_grads, axis=0, keepdims=True)
        weights[:, at] = grown
        grads[:, at] = prob_grads
        for k in range(tiles):
            part = slice(k * LANES, (k + 1) * LANES)
            for n, value in enumerate((top, total, dotted)):
                stats_all[me, n, pl.ds(g * tiles + k, 1)] = value[:, part]

    @pl.loop(first, n_groups + 1)
    def _(g):
        @pl.when(g < n_groups)
        def _():
            for k in range(n_groups // 2):
                b = g * group + 2 * k + core

                @pl.when(b > me)
                def _():
                    rows_copy(0, b).wait_recv()
                    pass_copy(b).start()

        @pl.when(g > first)
        def _():
            compute(g - 1)

    def stats_copy(there, source):
        return push(
            stats_all.at[source],
            stats_all.at[source],
            stats_send.at[there],
            stats_recv.at[source],
            {"ctx": there},
        )

    @pl.loop(1, n_ctx)
    def _(i):
        stats_copy(lax.rem(me + i, n_ctx), me).start()

    hidden_load.wait()
    proj_load.wait()
    hidden_values = hidden[...].astype(F32)
    inverse = lax.rsqrt(jnp.mean(hidden_values * hidden_values, axis=1, keepdims=True) + EPSILON)
    gained = hidden_values * gain_ref[...]
    high = gained.astype(BF16)
    low = (gained - high.astype(F32)).astype(BF16)
    pulled = (nt_dot(high, proj_t[...]) + nt_dot(low, proj_t[...])) * (1.0 / width)

    @pl.loop(0, n_ctx)
    def _(i):
        @pl.when(i != me)
        def _():
            stats_copy(me, i).wait_recv()

    tops = stats_all[:, 0]
    peak = jnp.max(tops, axis=0)
    factors = jnp.exp(tops - peak[None])
    total = jnp.sum(stats_all[:, 1] * factors, axis=0)
    delta = jnp.sum(stats_all[:, 2] * factors, axis=0) / total
    share = jnp.exp(stats_all[me, 0] - peak) / total
    share_row = jnp.concatenate([share[n : n + 1] for n in range(share.shape[0])], axis=1)
    delta_row = jnp.concatenate([delta[n : n + 1] for n in range(delta.shape[0])], axis=1)

    def key_copy(there, source):
        return push(
            key_parts.at[there], key_all.at[source], key_send.at[there], key_recv.at[source], {"exp": there}
        )

    piece = key_count // n_exp
    step = 2 * piece
    steps = key_count // step

    @pl.loop(1, steps + 1)
    def _(turn):
        n = lax.rem(mine // 2 + turn, steps)
        at = pl.ds(pl.multiple_of(n * step, step), step)
        probs = weights[at, :] * share_row
        now = (probs * (grads[at, :] - delta_row)).astype(BF16)
        score_grads[at, :] = now
        flat = rows_all[...].reshape(n_ctx * per, rows_all.shape[2])
        through = jnp.dot(now, flat[:, :wide], preferred_element_type=F32) * scale
        value = jnp.dot(probs.astype(BF16), flat[:, wide:], preferred_element_type=F32)
        for k in range(2):
            part = slice(k * piece, (k + 1) * piece)
            key_parts[2 * n + k, :, :value_width] = (
                through[part, :value_width] + value[part]
            ).astype(BF16)
            key_parts[2 * n + k, :, value_width:] = through[part, value_width:].astype(BF16)

            @pl.when(2 * n + k != mine)
            def _():
                key_copy(2 * n + k, mine).start()

    key_all[mine] = key_parts[mine]

    @pl.loop(0, n_groups)
    def _(g):
        at = pl.ds(pl.multiple_of(g * cols, cols), cols)
        part = tn_dot(score_grads[:, at], keys[...]) * scale
        parts = part.astype(BF16).reshape(group, per, wide)
        for k in range(group):
            query_out[k % 2, g * (group // 2) + k // 2] = parts[k]

    @pl.loop(0, n_exp)
    def _(s):
        @pl.when(s != mine)
        def _():
            key_copy(mine, s).wait_recv()

    key_total = key_all[0].astype(F32)
    for s in range(1, n_exp):
        key_total = key_total + key_all[s].astype(F32)
    key_rows = key_total.astype(BF16)
    aligned = jnp.sum(key_rows.astype(F32) * pulled, axis=1, keepdims=True)
    back = inverse * inverse * inverse * aligned
    stream_load.wait()
    depth = 512

    @pl.loop(0, width // depth)
    def _(c):
        at = pl.ds(pl.multiple_of(c * depth, depth), depth)
        norm_grad = jnp.dot(key_rows, proj_t[:, at], preferred_element_type=F32)
        through_norm = inverse * (gain_ref[:, at] * norm_grad) - hidden[:, at].astype(F32) * back
        stream_out[:, at] = (stream[:, at].astype(F32) + through_norm).astype(BF16)

    @pl.loop(0, me // 2)
    def _(i):
        rows_copy(me - 2 - 2 * i, me).wait_send()

    @pl.when(core == 1)
    def _():
        pass_copy(me).wait_send()

    @pl.loop(0, n_ctx // 2)
    def _(i):
        b = 2 * i + core

        @pl.when(b > me)
        def _():
            pass_copy(b).wait_send()

    @pl.loop(1, n_ctx)
    def _(i):
        stats_copy(lax.rem(me + i, n_ctx), me).wait_send()

    @pl.loop(0, n_exp)
    def _(s):
        @pl.when(s != mine)
        def _():
            key_copy(s, mine).wait_send()


def attention(queries, latents, out_grad, hidden_rows, norm_gain, latent_proj, stream_grad):
    key_count, key_width = latents.shape
    query_rows = queries.shape[0]
    heads = queries.shape[1] // key_width
    value_width = out_grad.shape[1] // heads
    per = query_rows * heads
    wide = padded(key_width)
    n_ctx, n_exp = lax.axis_size("ctx"), lax.axis_size("exp")
    piece = key_count // n_exp
    total_rows = n_ctx * per
    token_rows, width = hidden_rows.shape
    sizes = (n_ctx, n_exp, key_width, value_width, query_rows, heads)
    vmem = pl.BlockSpec(memory_space=pltpu.VMEM)
    hbm = pl.BlockSpec(memory_space=pl.ANY)
    dma = pltpu.SemaphoreType.DMA
    return pl.pallas_call(
        functools.partial(attention_kernel, sizes),
        out_shape=(
            jax.ShapeDtypeStruct((token_rows, width), BF16),
            jax.ShapeDtypeStruct((2, n_ctx // 2, per, wide), BF16),
        ),
        in_specs=[vmem, vmem, vmem, vmem, hbm, hbm, hbm],
        out_specs=(vmem, vmem),
        scratch_shapes=[
            pltpu.VMEM((n_ctx, per, wide + value_width), BF16),
            pltpu.VMEM((n_ctx, 3, total_rows // LANES, LANES), F32),
            pltpu.VMEM((key_count, wide), BF16),
            pltpu.VMEM((key_count, total_rows), F32),
            pltpu.VMEM((key_count, total_rows), F32),
            pltpu.VMEM((key_count, total_rows), BF16),
            pltpu.VMEM((n_exp, piece, wide), BF16),
            pltpu.VMEM((n_exp, piece, wide), BF16),
            pltpu.VMEM((token_rows, width), BF16),
            pltpu.VMEM((token_rows, width), BF16),
            pltpu.VMEM((wide, width), BF16),
            dma((3,)),
            dma((n_ctx,)),
            dma((n_ctx,)),
            dma((n_ctx,)),
            dma((n_ctx,)),
            dma((n_ctx,)),
            dma((n_exp,)),
            dma((n_exp,)),
        ],
        compiler_params=pltpu.CompilerParams(
            collective_id=0, has_side_effects=True, vmem_limit_bytes=58 * 2**20
        ),
    )(
        queries,
        out_grad,
        latents.T,
        norm_gain.reshape(1, width),
        hidden_rows,
        stream_grad,
        latent_proj.T,
    )


def expert_kernel(
    sizes,
    stream_ref,
    query_ref,
    ids_ref,
    route_ref,
    acts_ref,
    proj_hbm,
    act_out,
    down_out,
    weight_out,
    query_out,
    proj,
    placing,
    slot_weights,
    returned,
    query_in,
    query_sum,
    query_all,
    outgoing,
    arrived,
    weights_in,
    acts_t,
    through,
    partial,
    core_in,
    x_in,
    z_part,
    z_in,
    slot_parts,
    proj_sem,
    slot_send,
    slot_recv,
    weight_send,
    weight_recv,
    core_send,
    core_recv,
    x_send,
    x_recv,
    z_send,
    z_recv,
    back_send,
    back_recv,
    pair_send,
    pair_recv,
    query_send,
    query_recv,
):
    n_ctx, n_exp, chunks, n_x, n_z, key_width, window, lags = sizes
    me = lax.axis_index("ctx")
    mine = lax.axis_index("exp")
    core = lax.rem(me, 2)
    z_at = lax.rem(me // 2, n_z)
    x_at = me // (2 * n_z)
    depth = stream_ref.shape[1] // chunks
    slots, inner = acts_ref.shape
    capacity = slots // n_exp
    chips = n_ctx // 2
    share = inner // n_ctx

    def columns(c):
        return pl.ds(pl.multiple_of(c * depth, depth), depth)

    def proj_copy(c):
        return pltpu.make_async_copy(proj_hbm.at[:, columns(c)], proj.at[c], proj_sem.at[c])

    @pl.loop(0, chunks)
    def _(c):
        proj_copy(c).start()

    chip = me // 2
    meet(
        [{"exp": lax.rem(mine + k, n_exp)} for k in range(1, n_exp)]
        + [{"ctx": me + 1 - 2 * core}]
        + [{"ctx": lax.rem(me + 2 * k, n_ctx)} for k in range(1, chips)]
    )

    ids, route = ids_ref[...], route_ref[...].astype(BF16).astype(F32)
    tokens = ids.shape[1]
    expert = lax.broadcasted_iota(jnp.int32, (n_exp, tokens), 0)
    named = [expert == ids[k : k + 1] for k in range(ids.shape[0])]
    chosen = sum(n.astype(F32) for n in named)
    weight_of = sum(jnp.where(n, route[k : k + 1], 0.0) for k, n in enumerate(named))
    before = lax.broadcasted_iota(jnp.int32, (tokens, tokens), 0) < lax.broadcasted_iota(
        jnp.int32, (tokens, tokens), 1
    )
    rank = jnp.dot(chosen, before.astype(F32), preferred_element_type=F32).astype(jnp.int32)
    rank = jnp.where(chosen > 0, rank, -1)
    place = (
        rank[:, None, :] == lax.broadcasted_iota(jnp.int32, (n_exp, capacity, tokens), 1)
    ).astype(F32)
    placing[...] = place.reshape(slots, tokens).astype(BF16)
    slot_weights[...] = jnp.broadcast_to(
        jnp.sum(place * weight_of[:, None, :], axis=2, keepdims=True), slot_weights.shape
    ).astype(BF16)

    def pair_copy():
        return push(
            query_ref.at[1 - core], query_in, pair_send.at[0], pair_recv.at[0], {"ctx": me + 1 - 2 * core}
        )

    def query_copy(there, source):
        return push(
            query_sum.at[there],
            query_all.at[source],
            query_send.at[there],
            query_recv.at[source],
            {"ctx": there * 2 + core},
        )

    def weight_copy(there, source):
        return push(
            slot_weights.at[there],
            weights_in.at[source],
            weight_send.at[there],
            weight_recv.at[source],
            {"exp": there},
        )

    def slot_copy(c, there, source):
        return push(
            outgoing.at[c, there],
            arrived.at[c, source],
            slot_send.at[c, there],
            slot_recv.at[c, source],
            {"exp": there},
        )

    def core_copy(c):
        return push(
            partial.at[c, 1 - core], core_in.at[c], core_send.at[c], core_recv.at[c], {"ctx": me + 1 - 2 * core}
        )

    def x_copy(c, there, source):
        return push(
            partial.at[c, core, there],
            x_in.at[c, source],
            x_send.at[c, there],
            x_recv.at[c, source],
            {"ctx": (there * n_z + z_at) * 2 + core},
        )

    def z_copy(c):
        return push(
            z_part.at[c, 1 - z_at],
            z_in.at[c],
            z_send.at[c],
            z_recv.at[c],
            {"ctx": (x_at * n_z + 1 - z_at) * 2 + core},
        )

    def back_copy(there, source):
        return push(
            slot_parts.at[there], returned.at[source], back_send.at[there], back_recv.at[source], {"exp": there}
        )

    def send_slots(c):
        @pl.loop(1, n_exp)
        def _(k):
            slot_copy(c, lax.rem(mine + k, n_exp), mine).start()

    @pl.loop(1, n_exp)
    def _(k):
        weight_copy(lax.rem(mine + k, n_exp), mine).start()

    weights_in[mine] = slot_weights[mine]

    @pl.loop(0, chunks)
    def _(c):
        placed = jnp.dot(placing[...], stream_ref[:, columns(c)], preferred_element_type=F32)
        outgoing[c] = placed.astype(BF16).reshape(n_exp, capacity, depth)

        @pl.when(c < window)
        def _():
            send_slots(c)

        arrived[c, mine] = outgoing[c, mine]

    @pl.loop(1, n_exp)
    def _(k):
        weight_copy(mine, lax.rem(mine + k, n_exp)).wait_recv()

    slot_weight = weights_in[...].reshape(slots, LANES).astype(F32)[:, :1]
    turned = (acts_ref[...].astype(F32) * slot_weight).T.astype(BF16)
    for q in range(chips):
        for s in range(2):
            at = (q * 2 + s) * share
            to = (s * chips + q) * share
            acts_t[to : to + share] = turned[at : at + share]

    through[...] = jnp.zeros(through.shape, F32)

    lag1, lag2, lag3 = lags

    @pl.loop(0, chunks + lag3)
    def _(c):
        @pl.when(c < chunks)
        def _():
            @pl.loop(1, n_exp)
            def _(k):
                slot_copy(c, mine, lax.rem(mine + k, n_exp)).wait_recv()

            @pl.when(c + window < chunks)
            def _():
                send_slots(c + window)

            proj_copy(c).wait()
            rows = arrived[c].reshape(slots, depth)
            down = jnp.dot(acts_t[...], rows, preferred_element_type=F32)
            partial[c] = down.astype(BF16).reshape(2, n_x, n_z, share, depth)
            core_copy(c).start()
            through[...] += nt_dot(rows, proj[c])

        @pl.when((c >= lag1) & (c < chunks + lag1))
        def _():
            d = c - lag1
            core_copy(d).wait_recv()
            total = partial[d, core].astype(F32) + core_in[d].astype(F32)
            partial[d, core] = total.astype(BF16)
            x_in[d, x_at] = partial[d, core, x_at]

            @pl.loop(1, n_x)
            def _(k):
                x_copy(d, lax.rem(x_at + k, n_x), x_at).start()

        @pl.when((c >= lag2) & (c < chunks + lag2))
        def _():
            d = c - lag2

            @pl.loop(1, n_x)
            def _(k):
                x_copy(d, x_at, lax.rem(x_at + k, n_x)).wait_recv()

            total = x_in[d, 0].astype(F32)
            for k in range(1, n_x):
                total = total + x_in[d, k].astype(F32)
            z_part[d] = total.astype(BF16)
            z_copy(d).start()

        @pl.when(c >= lag3)
        def _():
            d = c - lag3
            z_copy(d).wait_recv()
            total = z_part[d, z_at].astype(F32) + z_in[d].astype(F32)
            down_out[:, columns(d)] = total.astype(BF16)

        @pl.when(c == 1)
        def _():
            pair_copy().start()

        @pl.when(c == chunks // 2)
        def _():
            pair_copy().wait_recv()
            query_sum[...] = (query_ref[core].astype(F32) + query_in[...].astype(F32)).astype(BF16)

            @pl.loop(chip + 1, chips)
            def _(q):
                query_copy(q, chip).start()

        @pl.when(c == chunks - 1)
        def _():
            all_through = through[...]
            act_out[...] = (all_through * slot_weight).astype(BF16)
            sums = jnp.sum(acts_ref[...].astype(F32) * all_through, axis=1, keepdims=True)
            slot_parts[...] = jnp.broadcast_to(sums, (slots, LANES)).reshape(slot_parts.shape)

            @pl.loop(1, n_exp)
            def _(k):
                back_copy(lax.rem(mine + k, n_exp), mine).start()

            returned[mine] = slot_parts[mine]

    def add(p, so_far):
        query_copy(chip, p).wait_recv()
        return so_far + query_all[p].astype(F32)

    query_total = lax.fori_loop(0, chip, add, query_sum[chip].astype(F32))
    query_rows = query_out.shape[0]
    heads = query_out.shape[1] // key_width
    query_out[...] = jnp.concatenate(
        [query_total[h * query_rows : (h + 1) * query_rows, :key_width] for h in range(heads)], axis=1
    ).astype(BF16)

    @pl.loop(1, n_exp)
    def _(k):
        there = lax.rem(mine + k, n_exp)
        back_copy(mine, there).wait_recv()
        back_copy(there, mine).wait_send()
        weight_copy(there, mine).wait_send()

    moved = jnp.sum(
        placing[...].astype(F32).reshape(n_exp, capacity, tokens) * returned[...], axis=1
    )
    for k in range(ids_ref.shape[0]):
        weight_out[k : k + 1] = jnp.sum(
            jnp.where(expert == ids_ref[k : k + 1], moved, 0.0), axis=0, keepdims=True
        )

    pair_copy().wait_send()

    @pl.loop(chip + 1, chips)
    def _(q):
        query_copy(q, chip).wait_send()

    @pl.loop(0, chunks)
    def _(c):
        @pl.loop(1, n_exp)
        def _(k):
            slot_copy(c, lax.rem(mine + k, n_exp), mine).wait_send()

        core_copy(c).wait_send()

        @pl.loop(1, n_x)
        def _(k):
            x_copy(c, lax.rem(x_at + k, n_x), x_at).wait_send()

        z_copy(c).wait_send()


def experts(stream_total, query_parts, ids, route, acts, proj, key_width, query_rows):
    n_ctx, n_exp = lax.axis_size("ctx"), lax.axis_size("exp")
    slots, inner = acts.shape
    tokens, width = stream_total.shape
    top_count = ids.shape[1]
    capacity = slots // n_exp
    chunks = 10
    n_z = 2
    n_x = n_ctx // (2 * n_z)
    depth = width // chunks
    share = inner // n_ctx
    chips = n_ctx // 2
    per, wide = query_parts.shape[2:]
    vmem = pl.BlockSpec(memory_space=pltpu.VMEM)
    dma = pltpu.SemaphoreType.DMA
    sizes = (n_ctx, n_exp, chunks, n_x, n_z, key_width, 2, (1, 2, 3))
    return pl.pallas_call(
        functools.partial(expert_kernel, sizes),
        out_shape=(
            jax.ShapeDtypeStruct((slots, inner), BF16),
            jax.ShapeDtypeStruct((share, width), BF16),
            jax.ShapeDtypeStruct((top_count, tokens), F32),
            jax.ShapeDtypeStruct((query_rows, per // query_rows * key_width), BF16),
        ),
        in_specs=[vmem, vmem, vmem, vmem, vmem, pl.BlockSpec(memory_space=pl.ANY)],
        out_specs=(vmem, vmem, vmem, vmem),
        scratch_shapes=[
            pltpu.VMEM((chunks, inner, depth), BF16),
            pltpu.VMEM((slots, tokens), BF16),
            pltpu.VMEM((n_exp, capacity, LANES), BF16),
            pltpu.VMEM((n_exp, capacity, LANES), F32),
            pltpu.VMEM((chips, per, wide), BF16),
            pltpu.VMEM((chips, per, wide), BF16),
            pltpu.VMEM((chips, per, wide), BF16),
            pltpu.VMEM((chunks, n_exp, capacity, depth), BF16),
            pltpu.VMEM((chunks, n_exp, capacity, depth), BF16),
            pltpu.VMEM((n_exp, capacity, LANES), BF16),
            pltpu.VMEM((inner, slots), BF16),
            pltpu.VMEM((slots, inner), F32),
            pltpu.VMEM((chunks, 2, n_x, n_z, share, depth), BF16),
            pltpu.VMEM((chunks, n_x, n_z, share, depth), BF16),
            pltpu.VMEM((chunks, n_x, n_z, share, depth), BF16),
            pltpu.VMEM((chunks, n_z, share, depth), BF16),
            pltpu.VMEM((chunks, share, depth), BF16),
            pltpu.VMEM((n_exp, capacity, LANES), F32),
            dma((chunks,)),
            dma((chunks, n_exp)),
            dma((chunks, n_exp)),
            dma((n_exp,)),
            dma((n_exp,)),
            dma((chunks,)),
            dma((chunks,)),
            dma((chunks, n_x)),
            dma((chunks, n_x)),
            dma((chunks,)),
            dma((chunks,)),
            dma((n_exp,)),
            dma((n_exp,)),
            dma((1,)),
            dma((1,)),
            dma((chips,)),
            dma((chips,)),
        ],
        compiler_params=pltpu.CompilerParams(
            collective_id=1, has_side_effects=True, vmem_limit_bytes=61 * 2**20
        ),
    )(stream_total, query_parts, ids.T, route.T, acts, proj)


def body(
    queries,
    latents,
    out_grad,
    hidden_rows,
    norm_gain,
    latent_proj,
    stream_grad,
    expert_ids,
    route_weights,
    expert_acts,
    down_proj,
):
    stream_total, query_parts = attention(
        queries, latents, out_grad, hidden_rows, norm_gain, latent_proj, stream_grad
    )
    act_grad, down_share, weight_grad, query_grad = experts(
        stream_total,
        query_parts,
        expert_ids,
        route_weights,
        expert_acts[0],
        down_proj[0],
        latents.shape[1],
        queries.shape[0],
    )
    return (query_grad, stream_total, act_grad[None], down_share[None], weight_grad.T)


def solution(mesh):
    in_specs = (
        P("ctx", "exp"),
        P("ctx", None),
        P("ctx", "exp"),
        P(("ctx", "exp"), None),
        P(),
        P(),
        P(("ctx", "exp"), None),
        P(("ctx", "exp"), None),
        P(("ctx", "exp"), None),
        P("exp", "ctx", None),
        P("exp", None, None),
    )
    out_specs = (
        P("ctx", "exp"),
        P(("ctx", "exp"), None),
        P("exp", "ctx", None),
        P("exp", "ctx", None),
        P(("ctx", "exp"), None),
    )
    return jax.shard_map(body, mesh=mesh, in_specs=in_specs, out_specs=out_specs, check_vma=False)
```

```python
import functools
import jax
import jax.numpy as jnp
from jax import lax
from jax.experimental import pallas as pl
from jax.experimental.pallas import tpu as pltpu
from jax.sharding import PartitionSpec as P

EPSILON = 1e-06
NEG_LARGE = -1e30
MESH = pl.DeviceIdType.MESH
F32 = jnp.float32
BF16 = jnp.bfloat16
LANES = 128


def padded(width):
    return -(-width // LANES) * LANES


def nt_dot(a, b):
    return lax.dot_general(a, b, (((1,), (1,)), ((), ())), preferred_element_type=F32)


def tn_dot(a, b):
    return lax.dot_general(a, b, (((0,), (0,)), ((), ())), preferred_element_type=F32)


def push(src, dst, send, recv, where):
    return pltpu.make_async_remote_copy(
        src_ref=src, dst_ref=dst, send_sem=send, recv_sem=recv, device_id=where, device_id_type=MESH
    )


def greet(axes):
    barrier = pltpu.get_barrier_semaphore()
    total = 0
    for axis, count in axes:
        me = lax.axis_index(axis)

        @pl.loop(0, count)
        def _(i):
            @pl.when(i != me)
            def _():
                pl.semaphore_signal(barrier, inc=1, device_id={axis: i}, device_id_type=MESH)

        total += count - 1
    pl.semaphore_wait(barrier, total)


def meet(peers):
    barrier = pltpu.get_barrier_semaphore()
    for where in peers:
        pl.semaphore_signal(barrier, inc=1, device_id=where, device_id_type=MESH)
    pl.semaphore_wait(barrier, len(peers))


def attention_kernel(
    sizes,
    queries_ref,
    out_grad_ref,
    latents_t_ref,
    gain_ref,
    hidden_hbm,
    stream_hbm,
    proj_t_hbm,
    stream_out,
    query_out,
    rows_all,
    stats_all,
    keys,
    weights,
    grads,
    score_grads,
    key_parts,
    key_all,
    hidden,
    stream,
    proj_t,
    load_sem,
    rows_send,
    rows_recv,
    pass_send,
    stats_send,
    stats_recv,
    key_send,
    key_recv,
):
    n_ctx, n_exp, key_width, value_width, query_rows, heads = sizes
    wide = padded(key_width)
    me = lax.axis_index("ctx")
    mine = lax.axis_index("exp")
    core = lax.rem(me, 2)
    sibling = me + 1 - 2 * core
    key_count = latents_t_ref.shape[1]
    width = gain_ref.shape[1]
    per = query_rows * heads
    scale = key_width ** (-0.5)
    group = 4
    cols = group * per
    n_groups = n_ctx // group
    tiles = cols // LANES
    first = me // group

    hidden_load = pltpu.make_async_copy(hidden_hbm, hidden, load_sem.at[0])
    proj_load = pltpu.make_async_copy(proj_t_hbm, proj_t.at[:key_width], load_sem.at[1])
    stream_load = pltpu.make_async_copy(stream_hbm, stream, load_sem.at[2])
    for copy in (hidden_load, proj_load, stream_load):
        copy.start()

    query_values = queries_ref[...].astype(F32)
    grad_values = out_grad_ref[...].astype(F32)
    rows_all[me, :, :key_width] = jnp.concatenate(
        [query_values[:, h * key_width : (h + 1) * key_width] for h in range(heads)], axis=0
    ).astype(BF16)
    rows_all[me, :, key_width:wide] = jnp.zeros((per, wide - key_width), BF16)
    rows_all[me, :, wide:] = jnp.concatenate(
        [grad_values[:, h * value_width : (h + 1) * value_width] for h in range(heads)], axis=0
    ).astype(BF16)

    greet((("ctx", n_ctx), ("exp", n_exp)))

    def rows_copy(there, source):
        return push(
            rows_all.at[source],
            rows_all.at[source],
            rows_send.at[there],
            rows_recv.at[source],
            {"ctx": there},
        )

    def pass_copy(source):
        return push(
            rows_all.at[source],
            rows_all.at[source],
            pass_send.at[source],
            rows_recv.at[source],
            {"ctx": sibling},
        )

    @pl.loop(0, me // 2)
    def _(i):
        rows_copy(me - 2 - 2 * i, me).start()

    @pl.when(core == 1)
    def _():
        pass_copy(me).start()

    @pl.loop(0, me)
    def _(i):
        rows_all[i] = jnp.zeros(rows_all.shape[1:], BF16)

    keys[:, :key_width] = latents_t_ref[...].T
    keys[:, key_width:] = jnp.zeros((key_count, wide - key_width), BF16)
    proj_t[key_width:] = jnp.zeros((wide - key_width, width), BF16)
    stats_all[me, 0] = jnp.full(stats_all.shape[2:], NEG_LARGE, F32)
    stats_all[me, 1] = jnp.zeros(stats_all.shape[2:], F32)
    stats_all[me, 2] = jnp.zeros(stats_all.shape[2:], F32)

    @pl.loop(0, first)
    def _(g):
        at = pl.ds(pl.multiple_of(g * cols, cols), cols)
        weights[:, at] = jnp.zeros((key_count, cols), F32)
        grads[:, at] = jnp.zeros((key_count, cols), F32)

    def compute(g):
        for k in range(n_groups // 2):
            b = g * group + 2 * k + 1 - core

            @pl.when(b > me)
            def _():
                pass_copy(b).wait_recv()

        block = rows_all[pl.ds(g * group, group)].reshape(cols, rows_all.shape[2])
        at = pl.ds(pl.multiple_of(g * cols, cols), cols)
        scores = nt_dot(keys[...], block[:, :wide]) * scale
        prob_grads = nt_dot(keys[:, :value_width], block[:, wide:])
        column = lax.broadcasted_iota(jnp.int32, (1, cols), 1)
        last = (
            (g * group + column // per - me) * key_count
            + key_count
            - query_rows
            + column % query_rows
        )
        visible = lax.broadcasted_iota(jnp.int32, (key_count, cols), 0) <= last
        masked = jnp.where(visible, scores, NEG_LARGE)
        top = jnp.max(masked, axis=0, keepdims=True)
        grown = jnp.where(visible, jnp.exp(masked - top), 0.0)
        total = jnp.sum(grown, axis=0, keepdims=True)
        dotted = jnp.sum(grown * prob_grads, axis=0, keepdims=True)
        weights[:, at] = grown
        grads[:, at] = prob_grads
        for k in range(tiles):
            part = slice(k * LANES, (k + 1) * LANES)
            for n, value in enumerate((top, total, dotted)):
                stats_all[me, n, pl.ds(g * tiles + k, 1)] = value[:, part]

    @pl.loop(first, n_groups + 1)
    def _(g):
        @pl.when(g < n_groups)
        def _():
            for k in range(n_groups // 2):
                b = g * group + 2 * k + core

                @pl.when(b > me)
                def _():
                    rows_copy(0, b).wait_recv()
                    pass_copy(b).start()

        @pl.when(g > first)
        def _():
            compute(g - 1)

    def stats_copy(there, source):
        return push(
            stats_all.at[source],
            stats_all.at[source],
            stats_send.at[there],
            stats_recv.at[source],
            {"ctx": there},
        )

    @pl.loop(1, n_ctx)
    def _(i):
        stats_copy(lax.rem(me + i, n_ctx), me).start()

    hidden_load.wait()
    proj_load.wait()
    hidden_values = hidden[...].astype(F32)
    inverse = lax.rsqrt(jnp.mean(hidden_values * hidden_values, axis=1, keepdims=True) + EPSILON)
    gained = hidden_values * gain_ref[...]
    high = gained.astype(BF16)
    low = (gained - high.astype(F32)).astype(BF16)
    pulled = (nt_dot(high, proj_t[...]) + nt_dot(low, proj_t[...])) * (1.0 / width)

    @pl.loop(0, n_ctx)
    def _(i):
        @pl.when(i != me)
        def _():
            stats_copy(me, i).wait_recv()

    tops = stats_all[:, 0]
    peak = jnp.max(tops, axis=0)
    factors = jnp.exp(tops - peak[None])
    total = jnp.sum(stats_all[:, 1] * factors, axis=0)
    delta = jnp.sum(stats_all[:, 2] * factors, axis=0) / total
    share = jnp.exp(stats_all[me, 0] - peak) / total
    share_row = jnp.concatenate([share[n : n + 1] for n in range(share.shape[0])], axis=1)
    delta_row = jnp.concatenate([delta[n : n + 1] for n in range(delta.shape[0])], axis=1)

    def key_copy(there, source):
        return push(
            key_parts.at[there], key_all.at[source], key_send.at[there], key_recv.at[source], {"exp": there}
        )

    piece = key_count // n_exp
    step = 2 * piece
    steps = key_count // step

    @pl.loop(1, steps + 1)
    def _(turn):
        n = lax.rem(mine // 2 + turn, steps)
        at = pl.ds(pl.multiple_of(n * step, step), step)
        probs = weights[at, :] * share_row
        now = (probs * (grads[at, :] - delta_row)).astype(BF16)
        score_grads[at, :] = now
        flat = rows_all[...].reshape(n_ctx * per, rows_all.shape[2])
        through = jnp.dot(now, flat[:, :wide], preferred_element_type=F32) * scale
        value = jnp.dot(probs.astype(BF16), flat[:, wide:], preferred_element_type=F32)
        for k in range(2):
            part = slice(k * piece, (k + 1) * piece)
            key_parts[2 * n + k, :, :value_width] = (
                through[part, :value_width] + value[part]
            ).astype(BF16)
            key_parts[2 * n + k, :, value_width:] = through[part, value_width:].astype(BF16)

            @pl.when(2 * n + k != mine)
            def _():
                key_copy(2 * n + k, mine).start()

    key_all[mine] = key_parts[mine]

    @pl.loop(0, n_groups)
    def _(g):
        at = pl.ds(pl.multiple_of(g * cols, cols), cols)
        part = tn_dot(score_grads[:, at], keys[...]) * scale
        parts = part.astype(BF16).reshape(group, per, wide)
        for k in range(group):
            query_out[k % 2, g * (group // 2) + k // 2] = parts[k]

    @pl.loop(0, n_exp)
    def _(s):
        @pl.when(s != mine)
        def _():
            key_copy(mine, s).wait_recv()

    key_total = key_all[0].astype(F32)
    for s in range(1, n_exp):
        key_total = key_total + key_all[s].astype(F32)
    key_rows = key_total.astype(BF16)
    aligned = jnp.sum(key_rows.astype(F32) * pulled, axis=1, keepdims=True)
    back = inverse * inverse * inverse * aligned
    stream_load.wait()
    depth = 512

    @pl.loop(0, width // depth)
    def _(c):
        at = pl.ds(pl.multiple_of(c * depth, depth), depth)
        norm_grad = jnp.dot(key_rows, proj_t[:, at], preferred_element_type=F32)
        through_norm = inverse * (gain_ref[:, at] * norm_grad) - hidden[:, at].astype(F32) * back
        stream_out[:, at] = (stream[:, at].astype(F32) + through_norm).astype(BF16)

    @pl.loop(0, me // 2)
    def _(i):
        rows_copy(me - 2 - 2 * i, me).wait_send()

    @pl.when(core == 1)
    def _():
        pass_copy(me).wait_send()

    @pl.loop(0, n_ctx // 2)
    def _(i):
        b = 2 * i + core

        @pl.when(b > me)
        def _():
            pass_copy(b).wait_send()

    @pl.loop(1, n_ctx)
    def _(i):
        stats_copy(lax.rem(me + i, n_ctx), me).wait_send()

    @pl.loop(0, n_exp)
    def _(s):
        @pl.when(s != mine)
        def _():
            key_copy(s, mine).wait_send()


def attention(queries, latents, out_grad, hidden_rows, norm_gain, latent_proj, stream_grad):
    key_count, key_width = latents.shape
    query_rows = queries.shape[0]
    heads = queries.shape[1] // key_width
    value_width = out_grad.shape[1] // heads
    per = query_rows * heads
    wide = padded(key_width)
    n_ctx, n_exp = lax.axis_size("ctx"), lax.axis_size("exp")
    piece = key_count // n_exp
    total_rows = n_ctx * per
    token_rows, width = hidden_rows.shape
    sizes = (n_ctx, n_exp, key_width, value_width, query_rows, heads)
    vmem = pl.BlockSpec(memory_space=pltpu.VMEM)
    hbm = pl.BlockSpec(memory_space=pl.ANY)
    dma = pltpu.SemaphoreType.DMA
    return pl.pallas_call(
        functools.partial(attention_kernel, sizes),
        out_shape=(
            jax.ShapeDtypeStruct((token_rows, width), BF16),
            jax.ShapeDtypeStruct((2, n_ctx // 2, per, wide), BF16),
        ),
        in_specs=[vmem, vmem, vmem, vmem, hbm, hbm, hbm],
        out_specs=(vmem, vmem),
        scratch_shapes=[
            pltpu.VMEM((n_ctx, per, wide + value_width), BF16),
            pltpu.VMEM((n_ctx, 3, total_rows // LANES, LANES), F32),
            pltpu.VMEM((key_count, wide), BF16),
            pltpu.VMEM((key_count, total_rows), F32),
            pltpu.VMEM((key_count, total_rows), F32),
            pltpu.VMEM((key_count, total_rows), BF16),
            pltpu.VMEM((n_exp, piece, wide), BF16),
            pltpu.VMEM((n_exp, piece, wide), BF16),
            pltpu.VMEM((token_rows, width), BF16),
            pltpu.VMEM((token_rows, width), BF16),
            pltpu.VMEM((wide, width), BF16),
            dma((3,)),
            dma((n_ctx,)),
            dma((n_ctx,)),
            dma((n_ctx,)),
            dma((n_ctx,)),
            dma((n_ctx,)),
            dma((n_exp,)),
            dma((n_exp,)),
        ],
        compiler_params=pltpu.CompilerParams(
            collective_id=0, has_side_effects=True, vmem_limit_bytes=58 * 2**20
        ),
    )(
        queries,
        out_grad,
        latents.T,
        norm_gain.reshape(1, width),
        hidden_rows,
        stream_grad,
        latent_proj.T,
    )


def expert_kernel(
    sizes,
    stream_ref,
    query_ref,
    ids_ref,
    route_ref,
    acts_ref,
    proj_hbm,
    act_out,
    down_out,
    weight_out,
    query_out,
    proj,
    placing,
    peer_placing,
    peer_rows,
    slot_weights,
    returned,
    query_in,
    query_sum,
    query_all,
    outgoing,
    arrived,
    weights_in,
    acts_t,
    through,
    partial,
    core_in,
    x_in,
    z_part,
    z_in,
    slot_parts,
    proj_sem,
    place_send,
    place_recv,
    peer_send,
    peer_recv,
    slot_send,
    slot_recv,
    weight_send,
    weight_recv,
    core_send,
    core_recv,
    x_send,
    x_recv,
    z_send,
    z_recv,
    back_send,
    back_recv,
    pair_send,
    pair_recv,
    query_send,
    query_recv,
):
    n_ctx, n_exp, chunks, n_x, n_z, key_width, window, lags = sizes
    me = lax.axis_index("ctx")
    mine = lax.axis_index("exp")
    core = lax.rem(me, 2)
    z_at = lax.rem(me // 2, n_z)
    x_at = me // (2 * n_z)
    depth = stream_ref.shape[1] // chunks
    slots, inner = acts_ref.shape
    capacity = slots // n_exp
    chips = n_ctx // 2
    share = inner // n_ctx

    def columns(c):
        return pl.ds(pl.multiple_of(c * depth, depth), depth)

    def proj_copy(c):
        return pltpu.make_async_copy(proj_hbm.at[:, columns(c)], proj.at[c], proj_sem.at[c])

    @pl.loop(0, chunks)
    def _(c):
        proj_copy(c).start()

    chip = me // 2
    l_at, y_at = lax.rem(mine, 2), mine // 2
    n_y = n_exp // 2
    partner = mine + 1 - 2 * l_at

    def turned_index(e):
        return lax.rem(e, 2) * n_y + e // 2

    meet(
        [{"exp": lax.rem(mine + k, n_exp)} for k in range(1, n_exp)]
        + [{"ctx": me + 1 - 2 * core}]
        + [{"ctx": lax.rem(me + 2 * k, n_ctx)} for k in range(1, chips)]
    )

    ids, route = ids_ref[...], route_ref[...].astype(BF16).astype(F32)
    tokens = ids.shape[1]
    row = lax.broadcasted_iota(jnp.int32, (n_exp, tokens), 0)
    expert = row % n_y * 2 + row // n_y
    named = [expert == ids[k : k + 1] for k in range(ids.shape[0])]
    chosen = sum(n.astype(F32) for n in named)
    weight_of = sum(jnp.where(n, route[k : k + 1], 0.0) for k, n in enumerate(named))
    before = lax.broadcasted_iota(jnp.int32, (tokens, tokens), 0) < lax.broadcasted_iota(
        jnp.int32, (tokens, tokens), 1
    )
    rank = jnp.dot(chosen, before.astype(F32), preferred_element_type=F32).astype(jnp.int32)
    rank = jnp.where(chosen > 0, rank, -1)
    place = (
        rank[:, None, :] == lax.broadcasted_iota(jnp.int32, (n_exp, capacity, tokens), 1)
    ).astype(F32)
    placing[...] = place.reshape(2, slots // 2, tokens).astype(BF16)
    slot_weights[...] = jnp.broadcast_to(
        jnp.sum(place * weight_of[:, None, :], axis=2, keepdims=True), slot_weights.shape
    ).astype(BF16)

    def pair_copy():
        return push(
            query_ref.at[1 - core], query_in, pair_send.at[0], pair_recv.at[0], {"ctx": me + 1 - 2 * core}
        )

    def query_copy(there, source):
        return push(
            query_sum.at[there],
            query_all.at[source],
            query_send.at[there],
            query_recv.at[source],
            {"ctx": there * 2 + core},
        )

    def weight_copy(there, source):
        return push(
            slot_weights.at[turned_index(there)],
            weights_in.at[source],
            weight_send.at[there],
            weight_recv.at[source],
            {"exp": there},
        )

    def slot_copy(c, k, there, source):
        return push(
            outgoing.at[c, k, there],
            arrived.at[c, source],
            slot_send.at[c, k, there],
            slot_recv.at[c, source],
            {"exp": there * 2 + l_at},
        )

    def core_copy(c):
        return push(
            partial.at[c, 1 - core], core_in.at[c], core_send.at[c], core_recv.at[c], {"ctx": me + 1 - 2 * core}
        )

    def x_copy(c, there, source):
        return push(
            partial.at[c, core, there],
            x_in.at[c, source],
            x_send.at[c, there],
            x_recv.at[c, source],
            {"ctx": (there * n_z + z_at) * 2 + core},
        )

    def z_copy(c):
        return push(
            z_part.at[c, 1 - z_at],
            z_in.at[c],
            z_send.at[c],
            z_recv.at[c],
            {"ctx": (x_at * n_z + 1 - z_at) * 2 + core},
        )

    def back_copy(there, source):
        return push(
            slot_parts.at[there], returned.at[turned_index(source)], back_send.at[there], back_recv.at[source], {"exp": there}
        )

    def place_copy():
        return push(
            placing.at[1 - l_at], peer_placing, place_send.at[0], place_recv.at[0], {"exp": partner}
        )

    def rows_copy(c):
        return push(
            stream_ref.at[:, columns(c)], peer_rows.at[c], peer_send.at[c], peer_recv.at[c], {"exp": partner}
        )

    def put_out(c, k, rows, place, source):
        placed = jnp.dot(place, rows, preferred_element_type=F32)
        outgoing[c, k] = placed.astype(BF16).reshape(n_y, capacity, depth)

        @pl.loop(1, n_y)
        def _(n):
            slot_copy(c, k, lax.rem(y_at + n, n_y), source).start()

        arrived[c, source] = outgoing[c, k, y_at]

    def send_slots(c):
        put_out(c, 0, stream_ref[:, columns(c)], placing[l_at], mine)
        rows_copy(c).wait_recv()
        put_out(c, 1, peer_rows[c], peer_placing[...], partner)

        @pl.when(c + ahead < chunks)
        def _():
            rows_copy(c + ahead).start()

    ahead = window + 2
    place_copy().start()
    for c in range(ahead):
        rows_copy(c).start()

    @pl.loop(1, n_exp)
    def _(k):
        weight_copy(lax.rem(mine + k, n_exp), mine).start()

    weights_in[mine] = slot_weights[turned_index(mine)]

    place_copy().wait_recv()
    for c in range(window):
        send_slots(c)

    @pl.loop(1, n_exp)
    def _(k):
        weight_copy(mine, lax.rem(mine + k, n_exp)).wait_recv()

    slot_weight = weights_in[...].reshape(slots, LANES).astype(F32)[:, :1]
    turned = (acts_ref[...].astype(F32) * slot_weight).T.astype(BF16)
    for q in range(chips):
        for s in range(2):
            at = (q * 2 + s) * share
            to = (s * chips + q) * share
            acts_t[to : to + share] = turned[at : at + share]

    through[...] = jnp.zeros(through.shape, F32)

    lag1, lag2, lag3 = lags

    @pl.loop(0, chunks + lag3)
    def _(c):
        @pl.when(c < chunks)
        def _():
            @pl.loop(1, n_y)
            def _(n):
                for k in range(2):
                    slot_copy(c, 0, y_at, lax.rem(y_at + n, n_y) * 2 + k).wait_recv()

            proj_copy(c).wait()
            rows = arrived[c].reshape(slots, depth)
            down = jnp.dot(acts_t[...], rows, preferred_element_type=F32)
            partial[c] = down.astype(BF16).reshape(2, n_x, n_z, share, depth)
            core_copy(c).start()
            through[...] += nt_dot(rows, proj[c])

        @pl.when((c >= lag1) & (c < chunks + lag1))
        def _():
            d = c - lag1
            core_copy(d).wait_recv()
            total = partial[d, core].astype(F32) + core_in[d].astype(F32)
            partial[d, core] = total.astype(BF16)
            x_in[d, x_at] = partial[d, core, x_at]

            @pl.loop(1, n_x)
            def _(k):
                x_copy(d, lax.rem(x_at + k, n_x), x_at).start()

        @pl.when((c >= lag2) & (c < chunks + lag2))
        def _():
            d = c - lag2

            @pl.loop(1, n_x)
            def _(k):
                x_copy(d, x_at, lax.rem(x_at + k, n_x)).wait_recv()

            total = x_in[d, 0].astype(F32)
            for k in range(1, n_x):
                total = total + x_in[d, k].astype(F32)
            z_part[d] = total.astype(BF16)
            z_copy(d).start()

        @pl.when(c >= lag3)
        def _():
            d = c - lag3
            z_copy(d).wait_recv()
            total = z_part[d, z_at].astype(F32) + z_in[d].astype(F32)
            down_out[:, columns(d)] = total.astype(BF16)

        @pl.when(c + window < chunks)
        def _():
            send_slots(c + window)

        @pl.when(c == 1)
        def _():
            pair_copy().start()

        @pl.when(c == chunks // 2)
        def _():
            pair_copy().wait_recv()
            query_sum[...] = (query_ref[core].astype(F32) + query_in[...].astype(F32)).astype(BF16)

            @pl.loop(chip + 1, chips)
            def _(q):
                query_copy(q, chip).start()

        @pl.when(c == chunks - 1)
        def _():
            all_through = through[...]
            act_out[...] = (all_through * slot_weight).astype(BF16)
            sums = jnp.sum(acts_ref[...].astype(F32) * all_through, axis=1, keepdims=True)
            slot_parts[...] = jnp.broadcast_to(sums, (slots, LANES)).reshape(slot_parts.shape)

            @pl.loop(1, n_exp)
            def _(k):
                back_copy(lax.rem(mine + k, n_exp), mine).start()

            returned[turned_index(mine)] = slot_parts[mine]

    def add(p, so_far):
        query_copy(chip, p).wait_recv()
        return so_far + query_all[p].astype(F32)

    query_total = lax.fori_loop(0, chip, add, query_sum[chip].astype(F32))
    query_rows = query_out.shape[0]
    heads = query_out.shape[1] // key_width
    query_out[...] = jnp.concatenate(
        [query_total[h * query_rows : (h + 1) * query_rows, :key_width] for h in range(heads)], axis=1
    ).astype(BF16)

    @pl.loop(1, n_exp)
    def _(k):
        there = lax.rem(mine + k, n_exp)
        back_copy(mine, there).wait_recv()
        back_copy(there, mine).wait_send()
        weight_copy(there, mine).wait_send()

    moved = jnp.sum(
        placing[...].astype(F32).reshape(n_exp, capacity, tokens) * returned[...], axis=1
    )
    for k in range(ids_ref.shape[0]):
        weight_out[k : k + 1] = jnp.sum(
            jnp.where(expert == ids_ref[k : k + 1], moved, 0.0), axis=0, keepdims=True
        )

    pair_copy().wait_send()
    place_copy().wait_send()

    @pl.loop(chip + 1, chips)
    def _(q):
        query_copy(q, chip).wait_send()

    @pl.loop(0, chunks)
    def _(c):
        rows_copy(c).wait_send()

        @pl.loop(1, n_y)
        def _(n):
            for k in range(2):
                slot_copy(c, k, lax.rem(y_at + n, n_y), mine).wait_send()

        core_copy(c).wait_send()

        @pl.loop(1, n_x)
        def _(k):
            x_copy(c, lax.rem(x_at + k, n_x), x_at).wait_send()

        z_copy(c).wait_send()


def experts(stream_total, query_parts, ids, route, acts, proj, key_width, query_rows):
    n_ctx, n_exp = lax.axis_size("ctx"), lax.axis_size("exp")
    slots, inner = acts.shape
    tokens, width = stream_total.shape
    top_count = ids.shape[1]
    capacity = slots // n_exp
    chunks = 10
    n_z = 2
    n_x = n_ctx // (2 * n_z)
    depth = width // chunks
    share = inner // n_ctx
    chips = n_ctx // 2
    per, wide = query_parts.shape[2:]
    vmem = pl.BlockSpec(memory_space=pltpu.VMEM)
    dma = pltpu.SemaphoreType.DMA
    sizes = (n_ctx, n_exp, chunks, n_x, n_z, key_width, 3, (1, 3, 5))
    return pl.pallas_call(
        functools.partial(expert_kernel, sizes),
        out_shape=(
            jax.ShapeDtypeStruct((slots, inner), BF16),
            jax.ShapeDtypeStruct((share, width), BF16),
            jax.ShapeDtypeStruct((top_count, tokens), F32),
            jax.ShapeDtypeStruct((query_rows, per // query_rows * key_width), BF16),
        ),
        in_specs=[vmem, vmem, vmem, vmem, vmem, pl.BlockSpec(memory_space=pl.ANY)],
        out_specs=(vmem, vmem, vmem, vmem),
        scratch_shapes=[
            pltpu.VMEM((chunks, inner, depth), BF16),
            pltpu.VMEM((2, slots // 2, tokens), BF16),
            pltpu.VMEM((slots // 2, tokens), BF16),
            pltpu.VMEM((chunks, tokens, depth), BF16),
            pltpu.VMEM((n_exp, capacity, LANES), BF16),
            pltpu.VMEM((n_exp, capacity, LANES), F32),
            pltpu.VMEM((chips, per, wide), BF16),
            pltpu.VMEM((chips, per, wide), BF16),
            pltpu.VMEM((chips, per, wide), BF16),
            pltpu.VMEM((chunks, 2, n_exp // 2, capacity, depth), BF16),
            pltpu.VMEM((chunks, n_exp, capacity, depth), BF16),
            pltpu.VMEM((n_exp, capacity, LANES), BF16),
            pltpu.VMEM((inner, slots), BF16),
            pltpu.VMEM((slots, inner), F32),
            pltpu.VMEM((chunks, 2, n_x, n_z, share, depth), BF16),
            pltpu.VMEM((chunks, n_x, n_z, share, depth), BF16),
            pltpu.VMEM((chunks, n_x, n_z, share, depth), BF16),
            pltpu.VMEM((chunks, n_z, share, depth), BF16),
            pltpu.VMEM((chunks, share, depth), BF16),
            pltpu.VMEM((n_exp, capacity, LANES), F32),
            dma((chunks,)),
            dma((1,)),
            dma((1,)),
            dma((chunks,)),
            dma((chunks,)),
            dma((chunks, 2, n_exp // 2)),
            dma((chunks, n_exp)),
            dma((n_exp,)),
            dma((n_exp,)),
            dma((chunks,)),
            dma((chunks,)),
            dma((chunks, n_x)),
            dma((chunks, n_x)),
            dma((chunks,)),
            dma((chunks,)),
            dma((n_exp,)),
            dma((n_exp,)),
            dma((1,)),
            dma((1,)),
            dma((chips,)),
            dma((chips,)),
        ],
        compiler_params=pltpu.CompilerParams(
            collective_id=1, has_side_effects=True, vmem_limit_bytes=61 * 2**20
        ),
    )(stream_total, query_parts, ids.T, route.T, acts, proj)


def body(
    queries,
    latents,
    out_grad,
    hidden_rows,
    norm_gain,
    latent_proj,
    stream_grad,
    expert_ids,
    route_weights,
    expert_acts,
    down_proj,
):
    stream_total, query_parts = attention(
        queries, latents, out_grad, hidden_rows, norm_gain, latent_proj, stream_grad
    )
    act_grad, down_share, weight_grad, query_grad = experts(
        stream_total,
        query_parts,
        expert_ids,
        route_weights,
        expert_acts[0],
        down_proj[0],
        latents.shape[1],
        queries.shape[0],
    )
    return (query_grad, stream_total, act_grad[None], down_share[None], weight_grad.T)


def solution(mesh):
    in_specs = (
        P("ctx", "exp"),
        P("ctx", None),
        P("ctx", "exp"),
        P(("ctx", "exp"), None),
        P(),
        P(),
        P(("ctx", "exp"), None),
        P(("ctx", "exp"), None),
        P(("ctx", "exp"), None),
        P("exp", "ctx", None),
        P("exp", None, None),
    )
    out_specs = (
        P("ctx", "exp"),
        P(("ctx", "exp"), None),
        P("exp", "ctx", None),
        P("exp", "ctx", None),
        P(("ctx", "exp"), None),
    )
    return jax.shard_map(body, mesh=mesh, in_specs=in_specs, out_specs=out_specs, check_vma=False)
```

```python
import functools
import jax
import jax.numpy as jnp
from jax import lax
from jax.experimental import pallas as pl
from jax.experimental.pallas import tpu as pltpu
from jax.sharding import PartitionSpec as P

EPSILON = 1e-06
LEAD = 2
NEG_LARGE = -1e30
MESH = pl.DeviceIdType.MESH
F32 = jnp.float32
BF16 = jnp.bfloat16
LANES = 128


def padded(width):
    return -(-width // LANES) * LANES


def nt_dot(a, b):
    return lax.dot_general(a, b, (((1,), (1,)), ((), ())), preferred_element_type=F32)


def tn_dot(a, b):
    return lax.dot_general(a, b, (((0,), (0,)), ((), ())), preferred_element_type=F32)


def push(src, dst, send, recv, where):
    return pltpu.make_async_remote_copy(
        src_ref=src, dst_ref=dst, send_sem=send, recv_sem=recv, device_id=where, device_id_type=MESH
    )


def greet(axes):
    barrier = pltpu.get_barrier_semaphore()
    total = 0
    for axis, count in axes:
        me = lax.axis_index(axis)

        @pl.loop(0, count)
        def _(i):
            @pl.when(i != me)
            def _():
                pl.semaphore_signal(barrier, inc=1, device_id={axis: i}, device_id_type=MESH)

        total += count - 1
    pl.semaphore_wait(barrier, total)


def attention_part(
    sizes,
    idle,
    ready,
    queries_ref,
    out_grad_ref,
    latents_t_ref,
    gain_ref,
    hidden_hbm,
    stream_hbm,
    proj_t_hbm,
    stream_out,
    query_out,
    rows_all,
    stats_all,
    keys,
    weights,
    grads,
    score_grads,
    key_parts,
    key_all,
    hidden,
    stream,
    proj_t,
    load_sem,
    rows_send,
    rows_recv,
    pass_send,
    stats_send,
    stats_recv,
    key_send,
    key_recv,
):
    n_ctx, n_exp, key_width, value_width, query_rows, heads, chunks = sizes
    wide = padded(key_width)
    me = lax.axis_index("ctx")
    mine = lax.axis_index("exp")
    core = lax.rem(me, 2)
    sibling = me + 1 - 2 * core
    key_count = latents_t_ref.shape[1]
    width = gain_ref.shape[1]
    per = query_rows * heads
    scale = key_width ** (-0.5)
    group = 4
    cols = group * per
    n_groups = n_ctx // group
    tiles = cols // LANES
    first = me // group

    hidden_load = pltpu.make_async_copy(hidden_hbm, hidden, load_sem.at[0])
    proj_load = pltpu.make_async_copy(proj_t_hbm, proj_t.at[:key_width], load_sem.at[1])
    stream_load = pltpu.make_async_copy(stream_hbm, stream, load_sem.at[2])
    query_values = queries_ref[...].astype(F32)
    grad_values = out_grad_ref[...].astype(F32)
    rows_all[me, :, :key_width] = jnp.concatenate(
        [query_values[:, h * key_width : (h + 1) * key_width] for h in range(heads)], axis=0
    ).astype(BF16)
    rows_all[me, :, key_width:wide] = jnp.zeros((per, wide - key_width), BF16)
    rows_all[me, :, wide:] = jnp.concatenate(
        [grad_values[:, h * value_width : (h + 1) * value_width] for h in range(heads)], axis=0
    ).astype(BF16)

    def rows_copy(there, source):
        return push(
            rows_all.at[source],
            rows_all.at[source],
            rows_send.at[there],
            rows_recv.at[source],
            {"ctx": there},
        )

    def pass_copy(source):
        return push(
            rows_all.at[source],
            rows_all.at[source],
            pass_send.at[source],
            rows_recv.at[source],
            {"ctx": sibling},
        )

    @pl.loop(0, me // 2)
    def _(i):
        rows_copy(me - 2 - 2 * i, me).start()

    @pl.when(core == 1)
    def _():
        pass_copy(me).start()

    for copy in (hidden_load, proj_load, stream_load):
        copy.start()

    @pl.loop(0, me)
    def _(i):
        rows_all[i] = jnp.zeros(rows_all.shape[1:], BF16)

    keys[:, :key_width] = latents_t_ref[...].T
    keys[:, key_width:] = jnp.zeros((key_count, wide - key_width), BF16)
    proj_t[key_width:] = jnp.zeros((wide - key_width, width), BF16)
    stats_all[me, 0] = jnp.full(stats_all.shape[2:], NEG_LARGE, F32)
    stats_all[me, 1] = jnp.zeros(stats_all.shape[2:], F32)
    stats_all[me, 2] = jnp.zeros(stats_all.shape[2:], F32)

    @pl.loop(0, first)
    def _(g):
        at = pl.ds(pl.multiple_of(g * cols, cols), cols)
        weights[:, at] = jnp.zeros((key_count, cols), F32)
        grads[:, at] = jnp.zeros((key_count, cols), F32)

    idle()

    def compute(g):
        for k in range(n_groups // 2):
            b = g * group + 2 * k + 1 - core

            @pl.when(b > me)
            def _():
                pass_copy(b).wait_recv()

        block = rows_all[pl.ds(g * group, group)].reshape(cols, rows_all.shape[2])
        at = pl.ds(pl.multiple_of(g * cols, cols), cols)
        scores = nt_dot(keys[...], block[:, :wide]) * scale
        prob_grads = nt_dot(keys[:, :value_width], block[:, wide:])
        column = lax.broadcasted_iota(jnp.int32, (1, cols), 1)
        last = (
            (g * group + column // per - me) * key_count
            + key_count
            - query_rows
            + column % query_rows
        )
        visible = lax.broadcasted_iota(jnp.int32, (key_count, cols), 0) <= last
        masked = jnp.where(visible, scores, NEG_LARGE)
        top = jnp.max(masked, axis=0, keepdims=True)
        grown = jnp.where(visible, jnp.exp(masked - top), 0.0)
        total = jnp.sum(grown, axis=0, keepdims=True)
        dotted = jnp.sum(grown * prob_grads, axis=0, keepdims=True)
        weights[:, at] = grown
        grads[:, at] = prob_grads
        for k in range(tiles):
            part = slice(k * LANES, (k + 1) * LANES)
            for n, value in enumerate((top, total, dotted)):
                stats_all[me, n, pl.ds(g * tiles + k, 1)] = value[:, part]

    @pl.loop(first, n_groups + 1)
    def _(g):
        @pl.when(g < n_groups)
        def _():
            for k in range(n_groups // 2):
                b = g * group + 2 * k + core

                @pl.when(b > me)
                def _():
                    rows_copy(0, b).wait_recv()
                    pass_copy(b).start()

        @pl.when(g > first)
        def _():
            compute(g - 1)

    def stats_copy(there, source):
        return push(
            stats_all.at[source],
            stats_all.at[source],
            stats_send.at[there],
            stats_recv.at[source],
            {"ctx": there},
        )

    @pl.loop(1, n_ctx)
    def _(i):
        stats_copy(lax.rem(me + i, n_ctx), me).start()

    hidden_load.wait()
    proj_load.wait()
    hidden_values = hidden[...].astype(F32)
    inverse = lax.rsqrt(jnp.mean(hidden_values * hidden_values, axis=1, keepdims=True) + EPSILON)
    gained = hidden_values * gain_ref[...]
    high = gained.astype(BF16)
    low = (gained - high.astype(F32)).astype(BF16)
    pulled = (nt_dot(high, proj_t[...]) + nt_dot(low, proj_t[...])) * (1.0 / width)

    @pl.loop(0, n_ctx)
    def _(i):
        @pl.when(i != me)
        def _():
            stats_copy(me, i).wait_recv()

    tops = stats_all[:, 0]
    peak = jnp.max(tops, axis=0)
    factors = jnp.exp(tops - peak[None])
    total = jnp.sum(stats_all[:, 1] * factors, axis=0)
    delta = jnp.sum(stats_all[:, 2] * factors, axis=0) / total
    share = jnp.exp(stats_all[me, 0] - peak) / total
    share_row = jnp.concatenate([share[n : n + 1] for n in range(share.shape[0])], axis=1)
    delta_row = jnp.concatenate([delta[n : n + 1] for n in range(delta.shape[0])], axis=1)

    def key_copy(there, source):
        return push(
            key_parts.at[there], key_all.at[source], key_send.at[there], key_recv.at[source], {"exp": there}
        )

    piece = key_count // n_exp
    step = 2 * piece
    steps = key_count // step

    @pl.loop(1, steps + 1)
    def _(turn):
        n = lax.rem(mine // 2 + turn, steps)
        at = pl.ds(pl.multiple_of(n * step, step), step)
        probs = weights[at, :] * share_row
        now = (probs * (grads[at, :] - delta_row)).astype(BF16)
        score_grads[at, :] = now
        flat = rows_all[...].reshape(n_ctx * per, rows_all.shape[2])
        through = jnp.dot(now, flat[:, :wide], preferred_element_type=F32) * scale
        value = jnp.dot(probs.astype(BF16), flat[:, wide:], preferred_element_type=F32)
        for k in range(2):
            part = slice(k * piece, (k + 1) * piece)
            key_parts[2 * n + k, :, :value_width] = (
                through[part, :value_width] + value[part]
            ).astype(BF16)
            key_parts[2 * n + k, :, value_width:] = through[part, value_width:].astype(BF16)

            @pl.when(2 * n + k != mine)
            def _():
                key_copy(2 * n + k, mine).start()

    key_all[mine] = key_parts[mine]

    @pl.loop(0, n_groups)
    def _(g):
        at = pl.ds(pl.multiple_of(g * cols, cols), cols)
        part = tn_dot(score_grads[:, at], keys[...]) * scale
        parts = part.astype(BF16).reshape(group, per, wide)
        for k in range(group):
            query_out[k % 2, g * (group // 2) + k // 2] = parts[k]

    @pl.loop(0, n_exp)
    def _(s):
        @pl.when(s != mine)
        def _():
            key_copy(mine, s).wait_recv()

    key_total = key_all[0].astype(F32)
    for s in range(1, n_exp):
        key_total = key_total + key_all[s].astype(F32)
    key_rows = key_total.astype(BF16)
    aligned = jnp.sum(key_rows.astype(F32) * pulled, axis=1, keepdims=True)
    back = inverse * inverse * inverse * aligned
    stream_load.wait()
    depth = width // chunks

    @pl.loop(0, width // depth)
    def _(c):
        at = pl.ds(pl.multiple_of(c * depth, depth), depth)
        norm_grad = jnp.dot(key_rows, proj_t[:, at], preferred_element_type=F32)
        through_norm = inverse * (gain_ref[:, at] * norm_grad) - hidden[:, at].astype(F32) * back
        stream_out[:, at] = (stream[:, at].astype(F32) + through_norm).astype(BF16)
        ready(c)

    @pl.loop(0, me // 2)
    def _(i):
        rows_copy(me - 2 - 2 * i, me).wait_send()

    @pl.when(core == 1)
    def _():
        pass_copy(me).wait_send()

    @pl.loop(0, n_ctx // 2)
    def _(i):
        b = 2 * i + core

        @pl.when(b > me)
        def _():
            pass_copy(b).wait_send()

    @pl.loop(1, n_ctx)
    def _(i):
        stats_copy(lax.rem(me + i, n_ctx), me).wait_send()

    @pl.loop(0, n_exp)
    def _(s):
        @pl.when(s != mine)
        def _():
            key_copy(s, mine).wait_send()


def expert_of_row(n_exp, tokens):
    row = lax.broadcasted_iota(jnp.int32, (n_exp, tokens), 0)
    return row % (n_exp // 2) * 2 + row // (n_exp // 2)


def slot_tables(ids_ref, route_ref, placing, slot_weights):
    n_exp, capacity = slot_weights.shape[:2]
    ids, route = ids_ref[...], route_ref[...].astype(BF16).astype(F32)
    tokens = ids.shape[1]
    expert = expert_of_row(n_exp, tokens)
    named = [expert == ids[k : k + 1] for k in range(ids.shape[0])]
    chosen = sum(n.astype(F32) for n in named)
    weight_of = sum(jnp.where(n, route[k : k + 1], 0.0) for k, n in enumerate(named))
    before = lax.broadcasted_iota(jnp.int32, (tokens, tokens), 0) < lax.broadcasted_iota(
        jnp.int32, (tokens, tokens), 1
    )
    rank = jnp.dot(chosen, before.astype(F32), preferred_element_type=F32).astype(jnp.int32)
    rank = jnp.where(chosen > 0, rank, -1)
    place = (
        rank[:, None, :] == lax.broadcasted_iota(jnp.int32, (n_exp, capacity, tokens), 1)
    ).astype(F32)
    placing[...] = place.reshape(placing.shape).astype(BF16)
    slot_weights[...] = jnp.broadcast_to(
        jnp.sum(place * weight_of[:, None, :], axis=2, keepdims=True), slot_weights.shape
    ).astype(BF16)


def expert_part(
    sizes,
    place_copy,
    rows_copy,
    weight_copy,
    stream_ref,
    query_ref,
    ids_ref,
    acts_ref,
    proj_hbm,
    act_out,
    down_out,
    weight_out,
    query_out,
    proj,
    placing,
    peer_placing,
    peer_rows,
    slot_weights,
    returned,
    query_in,
    query_sum,
    query_all,
    outgoing,
    arrived,
    weights_in,
    acts_t,
    through,
    partial,
    core_in,
    x_in,
    z_part,
    z_in,
    slot_parts,
    proj_sem,
    place_send,
    place_recv,
    peer_send,
    peer_recv,
    slot_send,
    slot_recv,
    weight_send,
    weight_recv,
    core_send,
    core_recv,
    x_send,
    x_recv,
    z_send,
    z_recv,
    back_send,
    back_recv,
    pair_send,
    pair_recv,
    query_send,
    query_recv,
):
    n_ctx, n_exp, chunks, n_x, n_z, key_width, window, lags = sizes
    me = lax.axis_index("ctx")
    mine = lax.axis_index("exp")
    core = lax.rem(me, 2)
    z_at = lax.rem(me // 2, n_z)
    x_at = me // (2 * n_z)
    depth = stream_ref.shape[1] // chunks
    slots, inner = acts_ref.shape
    capacity = slots // n_exp
    chips = n_ctx // 2
    share = inner // n_ctx

    def columns(c):
        return pl.ds(pl.multiple_of(c * depth, depth), depth)

    def proj_copy(c):
        return pltpu.make_async_copy(proj_hbm.at[:, columns(c)], proj.at[c], proj_sem.at[c])

    chip = me // 2
    l_at, y_at = lax.rem(mine, 2), mine // 2
    n_y = n_exp // 2
    partner = mine + 1 - 2 * l_at

    def turned_index(e):
        return lax.rem(e, 2) * n_y + e // 2

    tokens = ids_ref.shape[1]
    expert = expert_of_row(n_exp, tokens)

    def pair_copy():
        return push(
            query_ref.at[1 - core], query_in, pair_send.at[0], pair_recv.at[0], {"ctx": me + 1 - 2 * core}
        )

    def query_copy(there, source):
        return push(
            query_sum.at[there],
            query_all.at[source],
            query_send.at[there],
            query_recv.at[source],
            {"ctx": there * 2 + core},
        )

    def slot_copy(c, k, there, source):
        return push(
            outgoing.at[c, k, there],
            arrived.at[c, source],
            slot_send.at[c, k, there],
            slot_recv.at[c, source],
            {"exp": there * 2 + l_at},
        )

    def core_copy(c):
        return push(
            partial.at[c, 1 - core], core_in.at[c], core_send.at[c], core_recv.at[c], {"ctx": me + 1 - 2 * core}
        )

    def x_copy(c, there, source):
        return push(
            partial.at[c, core, there],
            x_in.at[c, source],
            x_send.at[c, there],
            x_recv.at[c, source],
            {"ctx": (there * n_z + z_at) * 2 + core},
        )

    def z_copy(c):
        return push(
            z_part.at[c, 1 - z_at],
            z_in.at[c],
            z_send.at[c],
            z_recv.at[c],
            {"ctx": (x_at * n_z + 1 - z_at) * 2 + core},
        )

    def back_copy(there, source):
        return push(
            slot_parts.at[there], returned.at[turned_index(source)], back_send.at[there], back_recv.at[source], {"exp": there}
        )

    def put_out(c, k, rows, place, source):
        placed = jnp.dot(place, rows, preferred_element_type=F32)
        outgoing[c, k] = placed.astype(BF16).reshape(n_y, capacity, depth)

        @pl.loop(1, n_y)
        def _(n):
            slot_copy(c, k, lax.rem(y_at + n, n_y), source).start()

        arrived[c, source] = outgoing[c, k, y_at]

    def send_slots(c):
        put_out(c, 0, stream_ref[:, columns(c)], placing[l_at], mine)
        rows_copy(c).wait_recv()
        put_out(c, 1, peer_rows[c], peer_placing[...], partner)

        @pl.when(c + ahead < chunks)
        def _():
            rows_copy(c + ahead).start()

    ahead = window + LEAD
    place_copy().wait_recv()
    for c in range(window):
        send_slots(c)

    @pl.loop(0, chunks)
    def _(c):
        proj_copy(c).start()

    @pl.loop(1, n_exp)
    def _(k):
        weight_copy(mine, lax.rem(mine + k, n_exp)).wait_recv()

    slot_weight = weights_in[...].reshape(slots, LANES).astype(F32)[:, :1]
    turned = (acts_ref[...].astype(F32) * slot_weight).T.astype(BF16)
    for q in range(chips):
        for s in range(2):
            at = (q * 2 + s) * share
            to = (s * chips + q) * share
            acts_t[to : to + share] = turned[at : at + share]

    through[...] = jnp.zeros(through.shape, F32)

    lag1, lag2, lag3 = lags

    @pl.loop(0, chunks + lag3)
    def _(c):
        @pl.when(c < chunks)
        def _():
            @pl.loop(1, n_y)
            def _(n):
                for k in range(2):
                    slot_copy(c, 0, y_at, lax.rem(y_at + n, n_y) * 2 + k).wait_recv()

            proj_copy(c).wait()
            rows = arrived[c].reshape(slots, depth)
            down = jnp.dot(acts_t[...], rows, preferred_element_type=F32)
            partial[c] = down.astype(BF16).reshape(2, n_x, n_z, share, depth)
            core_copy(c).start()
            through[...] += nt_dot(rows, proj[c])

        @pl.when((c >= lag1) & (c < chunks + lag1))
        def _():
            d = c - lag1
            core_copy(d).wait_recv()
            total = partial[d, core].astype(F32) + core_in[d].astype(F32)
            partial[d, core] = total.astype(BF16)
            x_in[d, x_at] = partial[d, core, x_at]

            @pl.loop(1, n_x)
            def _(k):
                x_copy(d, lax.rem(x_at + k, n_x), x_at).start()

        @pl.when((c >= lag2) & (c < chunks + lag2))
        def _():
            d = c - lag2

            @pl.loop(1, n_x)
            def _(k):
                x_copy(d, x_at, lax.rem(x_at + k, n_x)).wait_recv()

            total = x_in[d, 0].astype(F32)
            for k in range(1, n_x):
                total = total + x_in[d, k].astype(F32)
            z_part[d] = total.astype(BF16)
            z_copy(d).start()

        @pl.when(c >= lag3)
        def _():
            d = c - lag3
            z_copy(d).wait_recv()
            total = z_part[d, z_at].astype(F32) + z_in[d].astype(F32)
            down_out[:, columns(d)] = total.astype(BF16)

        @pl.when(c + window < chunks)
        def _():
            send_slots(c + window)

        @pl.when(c == 1)
        def _():
            pair_copy().start()

        @pl.when(c == chunks // 2)
        def _():
            pair_copy().wait_recv()
            query_sum[...] = (query_ref[core].astype(F32) + query_in[...].astype(F32)).astype(BF16)

            @pl.loop(chip + 1, chips)
            def _(q):
                query_copy(q, chip).start()

        @pl.when(c == chunks)
        def _():
            all_through = through[...]
            act_out[...] = (all_through * slot_weight).astype(BF16)
            sums = jnp.sum(acts_ref[...].astype(F32) * all_through, axis=1, keepdims=True)
            slot_parts[...] = jnp.broadcast_to(sums, (slots, LANES)).reshape(slot_parts.shape)

            @pl.loop(1, n_exp)
            def _(k):
                back_copy(lax.rem(mine + k, n_exp), mine).start()

            returned[turned_index(mine)] = slot_parts[mine]

    def add(p, so_far):
        query_copy(chip, p).wait_recv()
        return so_far + query_all[p].astype(F32)

    query_total = lax.fori_loop(0, chip, add, query_sum[chip].astype(F32))
    query_rows = query_out.shape[0]
    heads = query_out.shape[1] // key_width
    query_out[...] = jnp.concatenate(
        [query_total[h * query_rows : (h + 1) * query_rows, :key_width] for h in range(heads)], axis=1
    ).astype(BF16)

    @pl.loop(1, n_exp)
    def _(k):
        there = lax.rem(mine + k, n_exp)
        back_copy(mine, there).wait_recv()
        back_copy(there, mine).wait_send()
        weight_copy(there, mine).wait_send()

    moved = jnp.sum(
        placing[...].astype(F32).reshape(n_exp, capacity, tokens) * returned[...], axis=1
    )
    for k in range(ids_ref.shape[0]):
        weight_out[k : k + 1] = jnp.sum(
            jnp.where(expert == ids_ref[k : k + 1], moved, 0.0), axis=0, keepdims=True
        )

    pair_copy().wait_send()
    place_copy().wait_send()

    @pl.loop(chip + 1, chips)
    def _(q):
        query_copy(q, chip).wait_send()

    @pl.loop(0, chunks)
    def _(c):
        rows_copy(c).wait_send()

        @pl.loop(1, n_y)
        def _(n):
            for k in range(2):
                slot_copy(c, k, lax.rem(y_at + n, n_y), mine).wait_send()

        core_copy(c).wait_send()

        @pl.loop(1, n_x)
        def _(k):
            x_copy(c, lax.rem(x_at + k, n_x), x_at).wait_send()

        z_copy(c).wait_send()


def layer_kernel(sizes, *refs):
    attention_sizes, expert_sizes, shapes, counts = sizes
    refs = list(refs)

    def take(n):
        taken = refs[:n]
        del refs[:n]
        return taken

    queries, out_grad, latents_t, gain, hidden, stream, proj_t, ids, route, acts, proj = take(11)
    stream_out, act_out, down_out, weight_out, query_out = take(5)
    rows_all, stats_all, key_all, query_parts = take(4)
    placing, peer_placing, peer_rows, slot_weights, returned, query_in, query_sum, query_all = take(8)
    arrived, weights_in, core_in, x_in, z_in, slot_parts = take(6)
    attention_sems = take(counts[0])
    expert_sems = take(counts[1])
    greet((("ctx", attention_sizes[0]), ("exp", attention_sizes[1])))

    n_exp, chunks, window = attention_sizes[1], expert_sizes[2], expert_sizes[6]
    mine = lax.axis_index("exp")
    l_at = lax.rem(mine, 2)
    partner = {"exp": mine + 1 - 2 * l_at}
    depth = stream_out.shape[1] // chunks
    place_send, place_recv, peer_send, peer_recv = expert_sems[1:5]
    weight_send, weight_recv = expert_sems[7:9]

    def row_of(e):
        return lax.rem(e, 2) * (n_exp // 2) + e // 2

    def place_copy():
        return push(placing.at[1 - l_at], peer_placing, place_send.at[0], place_recv.at[0], partner)

    def rows_copy(c):
        columns = pl.ds(pl.multiple_of(c * depth, depth), depth)
        return push(stream_out.at[:, columns], peer_rows.at[c], peer_send.at[c], peer_recv.at[c], partner)

    def weight_copy(there, source):
        return push(
            slot_weights.at[row_of(there)],
            weights_in.at[source],
            weight_send.at[there],
            weight_recv.at[source],
            {"exp": there},
        )

    def idle():
        slot_tables(ids, route, placing, slot_weights)
        place_copy().start()

        @pl.loop(1, n_exp)
        def _(k):
            weight_copy(lax.rem(mine + k, n_exp), mine).start()

        weights_in[mine] = slot_weights[row_of(mine)]

    def ready(c):
        @pl.when(c < window + LEAD)
        def _():
            rows_copy(c).start()

    def first(keys, weights, grads, score_grads, key_parts, hidden_in, stream_in, proj_t_in):
        attention_part(
            attention_sizes,
            idle,
            ready,
            queries,
            out_grad,
            latents_t,
            gain,
            hidden,
            stream,
            proj_t,
            stream_out,
            query_parts,
            rows_all,
            stats_all,
            keys,
            weights,
            grads,
            score_grads,
            key_parts,
            key_all,
            hidden_in,
            stream_in,
            proj_t_in,
            *attention_sems,
        )

    def second(proj_in, outgoing, acts_t, through, partial, z_part):
        expert_part(
            expert_sizes,
            place_copy,
            rows_copy,
            weight_copy,
            stream_out,
            query_parts,
            ids,
            acts,
            proj,
            act_out,
            down_out,
            weight_out,
            query_out,
            proj_in,
            placing,
            peer_placing,
            peer_rows,
            slot_weights,
            returned,
            query_in,
            query_sum,
            query_all,
            outgoing,
            arrived,
            weights_in,
            acts_t,
            through,
            partial,
            core_in,
            x_in,
            z_part,
            z_in,
            slot_parts,
            *expert_sems,
        )

    pl.run_scoped(first, *shapes[0])
    pl.run_scoped(second, *shapes[1])


def layer(
    queries,
    latents,
    out_grad,
    hidden_rows,
    norm_gain,
    latent_proj,
    stream_grad,
    ids,
    route,
    acts,
    proj,
):
    n_ctx, n_exp = lax.axis_size("ctx"), lax.axis_size("exp")
    key_count, key_width = latents.shape
    query_rows = queries.shape[0]
    heads = queries.shape[1] // key_width
    value_width = out_grad.shape[1] // heads
    per = query_rows * heads
    wide = padded(key_width)
    piece = key_count // n_exp
    total_rows = n_ctx * per
    tokens, width = hidden_rows.shape
    slots, inner = acts.shape
    top_count = ids.shape[1]
    capacity = slots // n_exp
    chunks = 10
    n_z = 2
    n_x = n_ctx // (2 * n_z)
    depth = width // chunks
    share = inner // n_ctx
    chips = n_ctx // 2
    half = n_exp // 2
    vmem = pl.BlockSpec(memory_space=pltpu.VMEM)
    hbm = pl.BlockSpec(memory_space=pl.ANY)
    dma = pltpu.SemaphoreType.DMA
    attention_sizes = (n_ctx, n_exp, key_width, value_width, query_rows, heads, chunks)
    expert_sizes = (n_ctx, n_exp, chunks, n_x, n_z, key_width, 3, (1, 3, 5))
    first = (
        pltpu.VMEM((key_count, wide), BF16),
        pltpu.VMEM((key_count, total_rows), F32),
        pltpu.VMEM((key_count, total_rows), F32),
        pltpu.VMEM((key_count, total_rows), BF16),
        pltpu.VMEM((n_exp, piece, wide), BF16),
        pltpu.VMEM((tokens, width), BF16),
        pltpu.VMEM((tokens, width), BF16),
        pltpu.VMEM((wide, width), BF16),
    )
    second = (
        pltpu.VMEM((chunks, inner, depth), BF16),
        pltpu.VMEM((chunks, 2, half, capacity, depth), BF16),
        pltpu.VMEM((inner, slots), BF16),
        pltpu.VMEM((slots, inner), F32),
        pltpu.VMEM((chunks, 2, n_x, n_z, share, depth), BF16),
        pltpu.VMEM((chunks, n_z, share, depth), BF16),
    )
    held = [
        pltpu.VMEM((n_ctx, per, wide + value_width), BF16),
        pltpu.VMEM((n_ctx, 3, total_rows // LANES, LANES), F32),
        pltpu.VMEM((n_exp, piece, wide), BF16),
        pltpu.VMEM((2, chips, per, wide), BF16),
        pltpu.VMEM((2, slots // 2, tokens), BF16),
        pltpu.VMEM((slots // 2, tokens), BF16),
        pltpu.VMEM((chunks, tokens, depth), BF16),
        pltpu.VMEM((n_exp, capacity, LANES), BF16),
        pltpu.VMEM((n_exp, capacity, LANES), F32),
        pltpu.VMEM((chips, per, wide), BF16),
        pltpu.VMEM((chips, per, wide), BF16),
        pltpu.VMEM((chips, per, wide), BF16),
        pltpu.VMEM((chunks, n_exp, capacity, depth), BF16),
        pltpu.VMEM((n_exp, capacity, LANES), BF16),
        pltpu.VMEM((chunks, n_x, n_z, share, depth), BF16),
        pltpu.VMEM((chunks, n_x, n_z, share, depth), BF16),
        pltpu.VMEM((chunks, share, depth), BF16),
        pltpu.VMEM((n_exp, capacity, LANES), F32),
    ]
    attention_sems = [
        dma((3,)),
        dma((n_ctx,)),
        dma((n_ctx,)),
        dma((n_ctx,)),
        dma((n_ctx,)),
        dma((n_ctx,)),
        dma((n_exp,)),
        dma((n_exp,)),
    ]
    expert_sems = [
        dma((chunks,)),
        dma((1,)),
        dma((1,)),
        dma((chunks,)),
        dma((chunks,)),
        dma((chunks, 2, half)),
        dma((chunks, n_exp)),
        dma((n_exp,)),
        dma((n_exp,)),
        dma((chunks,)),
        dma((chunks,)),
        dma((chunks, n_x)),
        dma((chunks, n_x)),
        dma((chunks,)),
        dma((chunks,)),
        dma((n_exp,)),
        dma((n_exp,)),
        dma((1,)),
        dma((1,)),
        dma((chips,)),
        dma((chips,)),
    ]
    counts = (len(attention_sems), len(expert_sems))
    sizes = (attention_sizes, expert_sizes, (first, second), counts)
    return pl.pallas_call(
        functools.partial(layer_kernel, sizes),
        out_shape=(
            jax.ShapeDtypeStruct((tokens, width), BF16),
            jax.ShapeDtypeStruct((slots, inner), BF16),
            jax.ShapeDtypeStruct((share, width), BF16),
            jax.ShapeDtypeStruct((top_count, tokens), F32),
            jax.ShapeDtypeStruct((query_rows, heads * key_width), BF16),
        ),
        in_specs=[vmem, vmem, vmem, vmem, hbm, hbm, hbm, vmem, vmem, vmem, hbm],
        out_specs=(vmem, vmem, vmem, vmem, vmem),
        scratch_shapes=held + attention_sems + expert_sems,
        compiler_params=pltpu.CompilerParams(
            collective_id=0, has_side_effects=True, vmem_limit_bytes=62 * 2**20
        ),
    )(
        queries,
        out_grad,
        latents.T,
        norm_gain.reshape(1, width),
        hidden_rows,
        stream_grad,
        latent_proj.T,
        ids.T,
        route.T,
        acts,
        proj,
    )


def settle_kernel(*refs):
    count = (len(refs) - 2) // 3
    arrays, results, held = refs[:count], refs[count : 2 * count], refs[2 * count : 3 * count]
    in_sem, out_sem = refs[-2:]
    loads = [pltpu.make_async_copy(arrays[n], held[n], in_sem.at[n]) for n in range(count)]
    stores = [pltpu.make_async_copy(held[n], results[n], out_sem.at[n]) for n in range(count)]
    for n in range(count):
        loads[n].start()
    for n in range(count):
        loads[n].wait()
        stores[n].start()
    for n in range(count):
        stores[n].wait()


def settle(*arrays):
    hbm = pl.BlockSpec(memory_space=pl.ANY)
    sems = [pltpu.SemaphoreType.DMA((len(arrays),))] * 2
    return pl.pallas_call(
        settle_kernel,
        out_shape=tuple(jax.ShapeDtypeStruct(a.shape, a.dtype) for a in arrays),
        in_specs=[hbm] * len(arrays),
        out_specs=(hbm,) * len(arrays),
        scratch_shapes=[pltpu.VMEM(a.shape, a.dtype) for a in arrays] + sems,
    )(*arrays)


def body(
    queries,
    latents,
    out_grad,
    hidden_rows,
    norm_gain,
    latent_proj,
    stream_grad,
    expert_ids,
    route_weights,
    expert_acts,
    down_proj,
):
    stream_total, act_grad, down_share, weight_grad, query_grad = layer(
        queries,
        latents,
        out_grad,
        hidden_rows,
        norm_gain,
        latent_proj,
        stream_grad,
        expert_ids,
        route_weights,
        expert_acts[0],
        down_proj[0],
    )
    stream_total, act_grad, down_share, query_grad = settle(
        stream_total, act_grad, down_share, query_grad
    )
    return (query_grad, stream_total, act_grad[None], down_share[None], weight_grad.T)


def solution(mesh):
    in_specs = (
        P("ctx", "exp"),
        P("ctx", None),
        P("ctx", "exp"),
        P(("ctx", "exp"), None),
        P(),
        P(),
        P(("ctx", "exp"), None),
        P(("ctx", "exp"), None),
        P(("ctx", "exp"), None),
        P("exp", "ctx", None),
        P("exp", None, None),
    )
    out_specs = (
        P("ctx", "exp"),
        P(("ctx", "exp"), None),
        P("exp", "ctx", None),
        P("exp", "ctx", None),
        P(("ctx", "exp"), None),
    )
    return jax.shard_map(body, mesh=mesh, in_specs=in_specs, out_specs=out_specs, check_vma=False)
```

```python
import functools
import jax
import jax.numpy as jnp
from jax import lax
from jax.experimental import pallas as pl
from jax.experimental.pallas import tpu as pltpu
from jax.sharding import PartitionSpec as P

EPSILON = 1e-06
LEAD = 2
NEG_LARGE = -1e30
MESH = pl.DeviceIdType.MESH
F32 = jnp.float32
BF16 = jnp.bfloat16
LANES = 128


def padded(width):
    return -(-width // LANES) * LANES


def nt_dot(a, b):
    return lax.dot_general(a, b, (((1,), (1,)), ((), ())), preferred_element_type=F32)


def tn_dot(a, b):
    return lax.dot_general(a, b, (((0,), (0,)), ((), ())), preferred_element_type=F32)


def push(src, dst, send, recv, where):
    return pltpu.make_async_remote_copy(
        src_ref=src, dst_ref=dst, send_sem=send, recv_sem=recv, device_id=where, device_id_type=MESH
    )


def greet(axes):
    barrier = pltpu.get_barrier_semaphore()
    total = 0
    for axis, count in axes:
        me = lax.axis_index(axis)

        @pl.loop(0, count)
        def _(i):
            @pl.when(i != me)
            def _():
                pl.semaphore_signal(barrier, inc=1, device_id={axis: i}, device_id_type=MESH)

        total += count - 1
    pl.semaphore_wait(barrier, total)


def attention_part(
    sizes,
    idle,
    ready,
    queries_ref,
    out_grad_ref,
    latents_t_ref,
    gain_ref,
    hidden_hbm,
    stream_hbm,
    proj_t_hbm,
    stream_out,
    query_out,
    rows_all,
    stats_all,
    keys,
    weights,
    grads,
    score_grads,
    key_parts,
    key_all,
    hidden,
    stream,
    proj_t,
    squares,
    pulled_t,
    load_sem,
    rows_send,
    rows_recv,
    pass_send,
    stats_send,
    stats_recv,
    key_send,
    key_recv,
):
    n_ctx, n_exp, key_width, value_width, query_rows, heads, chunks = sizes
    wide = padded(key_width)
    me = lax.axis_index("ctx")
    mine = lax.axis_index("exp")
    core = lax.rem(me, 2)
    sibling = me + 1 - 2 * core
    key_count = latents_t_ref.shape[1]
    width = gain_ref.shape[1]
    per = query_rows * heads
    scale = key_width ** (-0.5)
    group = 4
    cols = group * per
    n_groups = n_ctx // group
    tiles = cols // LANES
    first = me // group

    hidden_load = pltpu.make_async_copy(hidden_hbm, hidden, load_sem.at[0])
    proj_load = pltpu.make_async_copy(proj_t_hbm, proj_t.at[:key_width], load_sem.at[1])
    stream_load = pltpu.make_async_copy(stream_hbm, stream, load_sem.at[2])
    query_values = queries_ref[...].astype(F32)
    grad_values = out_grad_ref[...].astype(F32)
    rows_all[me, :, :key_width] = jnp.concatenate(
        [query_values[:, h * key_width : (h + 1) * key_width] for h in range(heads)], axis=0
    ).astype(BF16)
    rows_all[me, :, key_width:wide] = jnp.zeros((per, wide - key_width), BF16)
    rows_all[me, :, wide:] = jnp.concatenate(
        [grad_values[:, h * value_width : (h + 1) * value_width] for h in range(heads)], axis=0
    ).astype(BF16)

    def rows_copy(there, source):
        return push(
            rows_all.at[source],
            rows_all.at[source],
            rows_send.at[there],
            rows_recv.at[source],
            {"ctx": there},
        )

    def pass_copy(source):
        return push(
            rows_all.at[source],
            rows_all.at[source],
            pass_send.at[source],
            rows_recv.at[source],
            {"ctx": sibling},
        )

    @pl.loop(0, me // 2)
    def _(i):
        rows_copy(me - 2 - 2 * i, me).start()

    @pl.when(core == 1)
    def _():
        pass_copy(me).start()

    for copy in (hidden_load, proj_load, stream_load):
        copy.start()

    @pl.loop(0, me)
    def _(i):
        rows_all[i] = jnp.zeros(rows_all.shape[1:], BF16)

    keys[:, :key_width] = latents_t_ref[...].T
    keys[:, key_width:] = jnp.zeros((key_count, wide - key_width), BF16)
    proj_t[key_width:] = jnp.zeros((wide - key_width, width), BF16)
    stats_all[me, 0] = jnp.full(stats_all.shape[2:], NEG_LARGE, F32)
    stats_all[me, 1] = jnp.zeros(stats_all.shape[2:], F32)
    stats_all[me, 2] = jnp.zeros(stats_all.shape[2:], F32)

    @pl.loop(0, first)
    def _(g):
        at = pl.ds(pl.multiple_of(g * cols, cols), cols)
        weights[:, at] = jnp.zeros((key_count, cols), F32)
        grads[:, at] = jnp.zeros((key_count, cols), F32)

    idle()

    def compute(g):
        for k in range(n_groups // 2):
            b = g * group + 2 * k + 1 - core

            @pl.when(b > me)
            def _():
                pass_copy(b).wait_recv()

        block = rows_all[pl.ds(g * group, group)].reshape(cols, rows_all.shape[2])
        at = pl.ds(pl.multiple_of(g * cols, cols), cols)
        scores = nt_dot(keys[...], block[:, :wide]) * scale
        prob_grads = nt_dot(keys[:, :value_width], block[:, wide:])
        column = lax.broadcasted_iota(jnp.int32, (1, cols), 1)
        last = (
            (g * group + column // per - me) * key_count
            + key_count
            - query_rows
            + column % query_rows
        )
        visible = lax.broadcasted_iota(jnp.int32, (key_count, cols), 0) <= last
        masked = jnp.where(visible, scores, NEG_LARGE)
        top = jnp.max(masked, axis=0, keepdims=True)
        grown = jnp.where(visible, jnp.exp(masked - top), 0.0)
        total = jnp.sum(grown, axis=0, keepdims=True)
        dotted = jnp.sum(grown * prob_grads, axis=0, keepdims=True)
        weights[:, at] = grown
        grads[:, at] = prob_grads
        for k in range(tiles):
            part = slice(k * LANES, (k + 1) * LANES)
            for n, value in enumerate((top, total, dotted)):
                stats_all[me, n, pl.ds(g * tiles + k, 1)] = value[:, part]

    span = width // n_groups
    tokens = hidden.shape[0]
    squares[...] = jnp.zeros(squares.shape, F32)
    pulled_t[...] = jnp.zeros(pulled_t.shape, F32)

    def pull(n):
        at = pl.ds(pl.multiple_of(n * span, span), span)
        values = hidden[:, at].astype(F32)
        squares[...] += jnp.broadcast_to(
            jnp.sum(values * values, axis=1, keepdims=True), squares.shape
        )
        gained = values * gain_ref[:, at]
        high = gained.astype(BF16)
        low = (gained - high.astype(F32)).astype(BF16)
        pulled_t[...] += nt_dot(proj_t[:, at], jnp.concatenate([high, low], axis=0))

    @pl.loop(first, n_groups + 1)
    def _(g):
        @pl.when(g < n_groups)
        def _():
            for k in range(n_groups // 2):
                b = g * group + 2 * k + core

                @pl.when(b > me)
                def _():
                    rows_copy(0, b).wait_recv()
                    pass_copy(b).start()

        @pl.when(g > first)
        def _():
            compute(g - 1)

    def stats_copy(there, source):
        return push(
            stats_all.at[source],
            stats_all.at[source],
            stats_send.at[there],
            stats_recv.at[source],
            {"ctx": there},
        )

    @pl.loop(1, n_ctx)
    def _(i):
        stats_copy(lax.rem(me + i, n_ctx), me).start()

    @pl.loop(0, n_ctx)
    def _(i):
        @pl.when(i != me)
        def _():
            stats_copy(me, i).wait_recv()

    tops = stats_all[:, 0]
    peak = jnp.max(tops, axis=0)
    factors = jnp.exp(tops - peak[None])
    total = jnp.sum(stats_all[:, 1] * factors, axis=0)
    delta = jnp.sum(stats_all[:, 2] * factors, axis=0) / total
    share = jnp.exp(stats_all[me, 0] - peak) / total
    share_row = jnp.concatenate([share[n : n + 1] for n in range(share.shape[0])], axis=1)
    delta_row = jnp.concatenate([delta[n : n + 1] for n in range(delta.shape[0])], axis=1)

    def key_copy(there, source):
        return push(
            key_parts.at[there], key_all.at[source], key_send.at[there], key_recv.at[source], {"exp": there}
        )

    piece = key_count // n_exp
    step = 2 * piece
    steps = key_count // step

    @pl.loop(1, steps + 1)
    def _(turn):
        n = lax.rem(mine // 2 + turn, steps)
        at = pl.ds(pl.multiple_of(n * step, step), step)
        probs = weights[at, :] * share_row
        now = (probs * (grads[at, :] - delta_row)).astype(BF16)
        score_grads[at, :] = now
        flat = rows_all[...].reshape(n_ctx * per, rows_all.shape[2])
        through = jnp.dot(now, flat[:, :wide], preferred_element_type=F32) * scale
        value = jnp.dot(probs.astype(BF16), flat[:, wide:], preferred_element_type=F32)
        for k in range(2):
            part = slice(k * piece, (k + 1) * piece)
            key_parts[2 * n + k, :, :value_width] = (
                through[part, :value_width] + value[part]
            ).astype(BF16)
            key_parts[2 * n + k, :, value_width:] = through[part, value_width:].astype(BF16)

            @pl.when(2 * n + k != mine)
            def _():
                key_copy(2 * n + k, mine).start()

    key_all[mine] = key_parts[mine]
    hidden_load.wait()
    proj_load.wait()

    @pl.loop(0, n_groups)
    def _(n):
        pull(n)

    @pl.loop(0, n_groups)
    def _(g):
        at = pl.ds(pl.multiple_of(g * cols, cols), cols)
        part = tn_dot(score_grads[:, at], keys[...]) * scale
        parts = part.astype(BF16).reshape(group, per, wide)
        for k in range(group):
            query_out[k % 2, g * (group // 2) + k // 2] = parts[k]

    inverse = lax.rsqrt(squares[:, :1] * (1.0 / width) + EPSILON)
    pulled = (pulled_t[:, :tokens] + pulled_t[:, tokens:]).T * (1.0 / width)

    @pl.loop(0, n_exp)
    def _(s):
        @pl.when(s != mine)
        def _():
            key_copy(mine, s).wait_recv()

    key_total = key_all[0].astype(F32)
    for s in range(1, n_exp):
        key_total = key_total + key_all[s].astype(F32)
    key_rows = key_total.astype(BF16)
    aligned = jnp.sum(key_rows.astype(F32) * pulled, axis=1, keepdims=True)
    back = inverse * inverse * inverse * aligned
    stream_load.wait()
    depth = width // chunks

    @pl.loop(0, width // depth)
    def _(c):
        at = pl.ds(pl.multiple_of(c * depth, depth), depth)
        norm_grad = jnp.dot(key_rows, proj_t[:, at], preferred_element_type=F32)
        through_norm = inverse * (gain_ref[:, at] * norm_grad) - hidden[:, at].astype(F32) * back
        stream_out[:, at] = (stream[:, at].astype(F32) + through_norm).astype(BF16)
        ready(c)

    @pl.loop(0, me // 2)
    def _(i):
        rows_copy(me - 2 - 2 * i, me).wait_send()

    @pl.when(core == 1)
    def _():
        pass_copy(me).wait_send()

    @pl.loop(0, n_ctx // 2)
    def _(i):
        b = 2 * i + core

        @pl.when(b > me)
        def _():
            pass_copy(b).wait_send()

    @pl.loop(1, n_ctx)
    def _(i):
        stats_copy(lax.rem(me + i, n_ctx), me).wait_send()

    @pl.loop(0, n_exp)
    def _(s):
        @pl.when(s != mine)
        def _():
            key_copy(s, mine).wait_send()


def expert_of_row(n_exp, tokens):
    row = lax.broadcasted_iota(jnp.int32, (n_exp, tokens), 0)
    return row % (n_exp // 2) * 2 + row // (n_exp // 2)


def slot_tables(ids_ref, route_ref, placing, slot_weights):
    n_exp, capacity = slot_weights.shape[:2]
    ids, route = ids_ref[...], route_ref[...].astype(BF16).astype(F32)
    tokens = ids.shape[1]
    expert = expert_of_row(n_exp, tokens)
    named = [expert == ids[k : k + 1] for k in range(ids.shape[0])]
    chosen = sum(n.astype(F32) for n in named)
    weight_of = sum(jnp.where(n, route[k : k + 1], 0.0) for k, n in enumerate(named))
    before = lax.broadcasted_iota(jnp.int32, (tokens, tokens), 0) < lax.broadcasted_iota(
        jnp.int32, (tokens, tokens), 1
    )
    rank = jnp.dot(chosen, before.astype(F32), preferred_element_type=F32).astype(jnp.int32)
    rank = jnp.where(chosen > 0, rank, -1)
    place = (
        rank[:, None, :] == lax.broadcasted_iota(jnp.int32, (n_exp, capacity, tokens), 1)
    ).astype(F32)
    placing[...] = place.reshape(placing.shape).astype(BF16)
    slot_weights[...] = jnp.broadcast_to(
        jnp.sum(place * weight_of[:, None, :], axis=2, keepdims=True), slot_weights.shape
    ).astype(BF16)


def expert_part(
    sizes,
    place_copy,
    rows_copy,
    weight_copy,
    stream_ref,
    query_ref,
    ids_ref,
    acts_ref,
    proj_hbm,
    act_out,
    down_out,
    weight_out,
    query_out,
    proj,
    placing,
    peer_placing,
    peer_rows,
    slot_weights,
    returned,
    query_in,
    query_sum,
    query_all,
    outgoing,
    arrived,
    weights_in,
    acts_t,
    through,
    partial,
    core_in,
    x_in,
    z_part,
    z_in,
    slot_parts,
    proj_sem,
    place_send,
    place_recv,
    peer_send,
    peer_recv,
    slot_send,
    slot_recv,
    weight_send,
    weight_recv,
    core_send,
    core_recv,
    x_send,
    x_recv,
    z_send,
    z_recv,
    back_send,
    back_recv,
    pair_send,
    pair_recv,
    query_send,
    query_recv,
):
    n_ctx, n_exp, chunks, n_x, n_z, key_width, window, lags = sizes
    me = lax.axis_index("ctx")
    mine = lax.axis_index("exp")
    core = lax.rem(me, 2)
    z_at = lax.rem(me // 2, n_z)
    x_at = me // (2 * n_z)
    depth = stream_ref.shape[1] // chunks
    slots, inner = acts_ref.shape
    capacity = slots // n_exp
    chips = n_ctx // 2
    share = inner // n_ctx

    def columns(c):
        return pl.ds(pl.multiple_of(c * depth, depth), depth)

    def proj_copy(c):
        return pltpu.make_async_copy(proj_hbm.at[:, columns(c)], proj.at[c], proj_sem.at[c])

    chip = me // 2
    l_at, y_at = lax.rem(mine, 2), mine // 2
    n_y = n_exp // 2
    partner = mine + 1 - 2 * l_at

    def turned_index(e):
        return lax.rem(e, 2) * n_y + e // 2

    tokens = ids_ref.shape[1]
    expert = expert_of_row(n_exp, tokens)

    def pair_copy():
        return push(
            query_ref.at[1 - core], query_in, pair_send.at[0], pair_recv.at[0], {"ctx": me + 1 - 2 * core}
        )

    def query_copy(there, source):
        return push(
            query_sum.at[there],
            query_all.at[source],
            query_send.at[there],
            query_recv.at[source],
            {"ctx": there * 2 + core},
        )

    def slot_copy(c, k, there, source):
        return push(
            outgoing.at[c, k, there],
            arrived.at[c, source],
            slot_send.at[c, k, there],
            slot_recv.at[c, source],
            {"exp": there * 2 + l_at},
        )

    def core_copy(c):
        return push(
            partial.at[c, 1 - core], core_in.at[c], core_send.at[c], core_recv.at[c], {"ctx": me + 1 - 2 * core}
        )

    def x_copy(c, there, source):
        return push(
            partial.at[c, core, there],
            x_in.at[c, source],
            x_send.at[c, there],
            x_recv.at[c, source],
            {"ctx": (there * n_z + z_at) * 2 + core},
        )

    def z_copy(c):
        return push(
            z_part.at[c, 1 - z_at],
            z_in.at[c],
            z_send.at[c],
            z_recv.at[c],
            {"ctx": (x_at * n_z + 1 - z_at) * 2 + core},
        )

    def back_copy(there, source):
        return push(
            slot_parts.at[there], returned.at[turned_index(source)], back_send.at[there], back_recv.at[source], {"exp": there}
        )

    def put_out(c, k, rows, place, source):
        placed = jnp.dot(place, rows, preferred_element_type=F32)
        outgoing[c, k] = placed.astype(BF16).reshape(n_y, capacity, depth)

        @pl.loop(1, n_y)
        def _(n):
            slot_copy(c, k, lax.rem(y_at + n, n_y), source).start()

        arrived[c, source] = outgoing[c, k, y_at]

    def send_slots(c):
        put_out(c, 0, stream_ref[:, columns(c)], placing[l_at], mine)
        rows_copy(c).wait_recv()
        put_out(c, 1, peer_rows[c], peer_placing[...], partner)

        @pl.when(c + ahead < chunks)
        def _():
            rows_copy(c + ahead).start()

    ahead = window + LEAD
    place_copy().wait_recv()
    for c in range(window):
        send_slots(c)

    @pl.loop(0, chunks)
    def _(c):
        proj_copy(c).start()

    @pl.loop(1, n_exp)
    def _(k):
        weight_copy(mine, lax.rem(mine + k, n_exp)).wait_recv()

    slot_weight = weights_in[...].reshape(slots, LANES).astype(F32)[:, :1]
    turned = (acts_ref[...].astype(F32) * slot_weight).T.astype(BF16)
    for q in range(chips):
        for s in range(2):
            at = (q * 2 + s) * share
            to = (s * chips + q) * share
            acts_t[to : to + share] = turned[at : at + share]

    through[...] = jnp.zeros(through.shape, F32)

    lag1, lag2, lag3 = lags

    @pl.loop(0, chunks + lag3)
    def _(c):
        @pl.when(c < chunks)
        def _():
            @pl.loop(1, n_y)
            def _(n):
                for k in range(2):
                    slot_copy(c, 0, y_at, lax.rem(y_at + n, n_y) * 2 + k).wait_recv()

            proj_copy(c).wait()
            rows = arrived[c].reshape(slots, depth)
            down = jnp.dot(acts_t[...], rows, preferred_element_type=F32)
            partial[c] = down.astype(BF16).reshape(2, n_x, n_z, share, depth)
            core_copy(c).start()
            through[...] += nt_dot(rows, proj[c])

        @pl.when((c >= lag1) & (c < chunks + lag1))
        def _():
            d = c - lag1
            core_copy(d).wait_recv()
            total = partial[d, core].astype(F32) + core_in[d].astype(F32)
            partial[d, core] = total.astype(BF16)
            x_in[d, x_at] = partial[d, core, x_at]

            @pl.loop(1, n_x)
            def _(k):
                x_copy(d, lax.rem(x_at + k, n_x), x_at).start()

        @pl.when((c >= lag2) & (c < chunks + lag2))
        def _():
            d = c - lag2

            @pl.loop(1, n_x)
            def _(k):
                x_copy(d, x_at, lax.rem(x_at + k, n_x)).wait_recv()

            total = x_in[d, 0].astype(F32)
            for k in range(1, n_x):
                total = total + x_in[d, k].astype(F32)
            z_part[d] = total.astype(BF16)
            z_copy(d).start()

        @pl.when(c >= lag3)
        def _():
            d = c - lag3
            z_copy(d).wait_recv()
            total = z_part[d, z_at].astype(F32) + z_in[d].astype(F32)
            down_out[:, columns(d)] = total.astype(BF16)

        @pl.when(c + window < chunks)
        def _():
            send_slots(c + window)

        @pl.when(c == 1)
        def _():
            pair_copy().start()

        @pl.when(c == chunks // 2)
        def _():
            pair_copy().wait_recv()
            query_sum[...] = (query_ref[core].astype(F32) + query_in[...].astype(F32)).astype(BF16)

            @pl.loop(chip + 1, chips)
            def _(q):
                query_copy(q, chip).start()

        @pl.when(c == chunks)
        def _():
            all_through = through[...]
            act_out[...] = (all_through * slot_weight).astype(BF16)
            sums = jnp.sum(acts_ref[...].astype(F32) * all_through, axis=1, keepdims=True)
            slot_parts[...] = jnp.broadcast_to(sums, (slots, LANES)).reshape(slot_parts.shape)

            @pl.loop(1, n_exp)
            def _(k):
                back_copy(lax.rem(mine + k, n_exp), mine).start()

            returned[turned_index(mine)] = slot_parts[mine]

    def add(p, so_far):
        query_copy(chip, p).wait_recv()
        return so_far + query_all[p].astype(F32)

    query_total = lax.fori_loop(0, chip, add, query_sum[chip].astype(F32))
    query_rows = query_out.shape[0]
    heads = query_out.shape[1] // key_width
    query_out[...] = jnp.concatenate(
        [query_total[h * query_rows : (h + 1) * query_rows, :key_width] for h in range(heads)], axis=1
    ).astype(BF16)

    @pl.loop(1, n_exp)
    def _(k):
        there = lax.rem(mine + k, n_exp)
        back_copy(mine, there).wait_recv()
        back_copy(there, mine).wait_send()
        weight_copy(there, mine).wait_send()

    moved = jnp.sum(
        placing[...].astype(F32).reshape(n_exp, capacity, tokens) * returned[...], axis=1
    )
    for k in range(ids_ref.shape[0]):
        weight_out[k : k + 1] = jnp.sum(
            jnp.where(expert == ids_ref[k : k + 1], moved, 0.0), axis=0, keepdims=True
        )

    pair_copy().wait_send()
    place_copy().wait_send()

    @pl.loop(chip + 1, chips)
    def _(q):
        query_copy(q, chip).wait_send()

    @pl.loop(0, chunks)
    def _(c):
        rows_copy(c).wait_send()

        @pl.loop(1, n_y)
        def _(n):
            for k in range(2):
                slot_copy(c, k, lax.rem(y_at + n, n_y), mine).wait_send()

        core_copy(c).wait_send()

        @pl.loop(1, n_x)
        def _(k):
            x_copy(c, lax.rem(x_at + k, n_x), x_at).wait_send()

        z_copy(c).wait_send()


def layer_kernel(sizes, *refs):
    attention_sizes, expert_sizes, shapes, counts = sizes
    refs = list(refs)

    def take(n):
        taken = refs[:n]
        del refs[:n]
        return taken

    queries, out_grad, latents_t, gain, hidden, stream, proj_t, ids, route, acts, proj = take(11)
    stream_out, act_out, down_out, weight_out, query_out = take(5)
    rows_all, stats_all, key_all, query_parts = take(4)
    placing, peer_placing, peer_rows, slot_weights, returned, query_in, query_sum, query_all = take(8)
    arrived, weights_in, core_in, x_in, z_in, slot_parts = take(6)
    attention_sems = take(counts[0])
    expert_sems = take(counts[1])
    greet((("ctx", attention_sizes[0]), ("exp", attention_sizes[1])))

    n_exp, chunks, window = attention_sizes[1], expert_sizes[2], expert_sizes[6]
    mine = lax.axis_index("exp")
    l_at = lax.rem(mine, 2)
    partner = {"exp": mine + 1 - 2 * l_at}
    depth = stream_out.shape[1] // chunks
    place_send, place_recv, peer_send, peer_recv = expert_sems[1:5]
    weight_send, weight_recv = expert_sems[7:9]

    def row_of(e):
        return lax.rem(e, 2) * (n_exp // 2) + e // 2

    def place_copy():
        return push(placing.at[1 - l_at], peer_placing, place_send.at[0], place_recv.at[0], partner)

    def rows_copy(c):
        columns = pl.ds(pl.multiple_of(c * depth, depth), depth)
        return push(stream_out.at[:, columns], peer_rows.at[c], peer_send.at[c], peer_recv.at[c], partner)

    def weight_copy(there, source):
        return push(
            slot_weights.at[row_of(there)],
            weights_in.at[source],
            weight_send.at[there],
            weight_recv.at[source],
            {"exp": there},
        )

    def idle():
        slot_tables(ids, route, placing, slot_weights)
        place_copy().start()

        @pl.loop(1, n_exp)
        def _(k):
            weight_copy(lax.rem(mine + k, n_exp), mine).start()

        weights_in[mine] = slot_weights[row_of(mine)]

    def ready(c):
        @pl.when(c < window + LEAD)
        def _():
            rows_copy(c).start()

    def first(
        keys, weights, grads, score_grads, key_parts, hidden_in, stream_in, proj_t_in, squares, pulled_t
    ):
        attention_part(
            attention_sizes,
            idle,
            ready,
            queries,
            out_grad,
            latents_t,
            gain,
            hidden,
            stream,
            proj_t,
            stream_out,
            query_parts,
            rows_all,
            stats_all,
            keys,
            weights,
            grads,
            score_grads,
            key_parts,
            key_all,
            hidden_in,
            stream_in,
            proj_t_in,
            squares,
            pulled_t,
            *attention_sems,
        )

    def second(proj_in, outgoing, acts_t, through, partial, z_part):
        expert_part(
            expert_sizes,
            place_copy,
            rows_copy,
            weight_copy,
            stream_out,
            query_parts,
            ids,
            acts,
            proj,
            act_out,
            down_out,
            weight_out,
            query_out,
            proj_in,
            placing,
            peer_placing,
            peer_rows,
            slot_weights,
            returned,
            query_in,
            query_sum,
            query_all,
            outgoing,
            arrived,
            weights_in,
            acts_t,
            through,
            partial,
            core_in,
            x_in,
            z_part,
            z_in,
            slot_parts,
            *expert_sems,
        )

    pl.run_scoped(first, *shapes[0])
    pl.run_scoped(second, *shapes[1])


def layer(
    queries,
    latents,
    out_grad,
    hidden_rows,
    norm_gain,
    latent_proj,
    stream_grad,
    ids,
    route,
    acts,
    proj,
):
    n_ctx, n_exp = lax.axis_size("ctx"), lax.axis_size("exp")
    key_count, key_width = latents.shape
    query_rows = queries.shape[0]
    heads = queries.shape[1] // key_width
    value_width = out_grad.shape[1] // heads
    per = query_rows * heads
    wide = padded(key_width)
    piece = key_count // n_exp
    total_rows = n_ctx * per
    tokens, width = hidden_rows.shape
    slots, inner = acts.shape
    top_count = ids.shape[1]
    capacity = slots // n_exp
    chunks = 10
    n_z = 2
    n_x = n_ctx // (2 * n_z)
    depth = width // chunks
    share = inner // n_ctx
    chips = n_ctx // 2
    half = n_exp // 2
    vmem = pl.BlockSpec(memory_space=pltpu.VMEM)
    hbm = pl.BlockSpec(memory_space=pl.ANY)
    dma = pltpu.SemaphoreType.DMA
    attention_sizes = (n_ctx, n_exp, key_width, value_width, query_rows, heads, chunks)
    expert_sizes = (n_ctx, n_exp, chunks, n_x, n_z, key_width, 3, (1, 3, 5))
    first = (
        pltpu.VMEM((key_count, wide), BF16),
        pltpu.VMEM((key_count, total_rows), F32),
        pltpu.VMEM((key_count, total_rows), F32),
        pltpu.VMEM((key_count, total_rows), BF16),
        pltpu.VMEM((n_exp, piece, wide), BF16),
        pltpu.VMEM((tokens, width), BF16),
        pltpu.VMEM((tokens, width), BF16),
        pltpu.VMEM((wide, width), BF16),
        pltpu.VMEM((tokens, LANES), F32),
        pltpu.VMEM((wide, 2 * tokens), F32),
    )
    second = (
        pltpu.VMEM((chunks, inner, depth), BF16),
        pltpu.VMEM((chunks, 2, half, capacity, depth), BF16),
        pltpu.VMEM((inner, slots), BF16),
        pltpu.VMEM((slots, inner), F32),
        pltpu.VMEM((chunks, 2, n_x, n_z, share, depth), BF16),
        pltpu.VMEM((chunks, n_z, share, depth), BF16),
    )
    held = [
        pltpu.VMEM((n_ctx, per, wide + value_width), BF16),
        pltpu.VMEM((n_ctx, 3, total_rows // LANES, LANES), F32),
        pltpu.VMEM((n_exp, piece, wide), BF16),
        pltpu.VMEM((2, chips, per, wide), BF16),
        pltpu.VMEM((2, slots // 2, tokens), BF16),
        pltpu.VMEM((slots // 2, tokens), BF16),
        pltpu.VMEM((chunks, tokens, depth), BF16),
        pltpu.VMEM((n_exp, capacity, LANES), BF16),
        pltpu.VMEM((n_exp, capacity, LANES), F32),
        pltpu.VMEM((chips, per, wide), BF16),
        pltpu.VMEM((chips, per, wide), BF16),
        pltpu.VMEM((chips, per, wide), BF16),
        pltpu.VMEM((chunks, n_exp, capacity, depth), BF16),
        pltpu.VMEM((n_exp, capacity, LANES), BF16),
        pltpu.VMEM((chunks, n_x, n_z, share, depth), BF16),
        pltpu.VMEM((chunks, n_x, n_z, share, depth), BF16),
        pltpu.VMEM((chunks, share, depth), BF16),
        pltpu.VMEM((n_exp, capacity, LANES), F32),
    ]
    attention_sems = [
        dma((3,)),
        dma((n_ctx,)),
        dma((n_ctx,)),
        dma((n_ctx,)),
        dma((n_ctx,)),
        dma((n_ctx,)),
        dma((n_exp,)),
        dma((n_exp,)),
    ]
    expert_sems = [
        dma((chunks,)),
        dma((1,)),
        dma((1,)),
        dma((chunks,)),
        dma((chunks,)),
        dma((chunks, 2, half)),
        dma((chunks, n_exp)),
        dma((n_exp,)),
        dma((n_exp,)),
        dma((chunks,)),
        dma((chunks,)),
        dma((chunks, n_x)),
        dma((chunks, n_x)),
        dma((chunks,)),
        dma((chunks,)),
        dma((n_exp,)),
        dma((n_exp,)),
        dma((1,)),
        dma((1,)),
        dma((chips,)),
        dma((chips,)),
    ]
    counts = (len(attention_sems), len(expert_sems))
    sizes = (attention_sizes, expert_sizes, (first, second), counts)
    return pl.pallas_call(
        functools.partial(layer_kernel, sizes),
        out_shape=(
            jax.ShapeDtypeStruct((tokens, width), BF16),
            jax.ShapeDtypeStruct((slots, inner), BF16),
            jax.ShapeDtypeStruct((share, width), BF16),
            jax.ShapeDtypeStruct((top_count, tokens), F32),
            jax.ShapeDtypeStruct((query_rows, heads * key_width), BF16),
        ),
        in_specs=[vmem, vmem, vmem, vmem, hbm, hbm, hbm, vmem, vmem, vmem, hbm],
        out_specs=(vmem, vmem, vmem, vmem, vmem),
        scratch_shapes=held + attention_sems + expert_sems,
        compiler_params=pltpu.CompilerParams(
            collective_id=0, has_side_effects=True, vmem_limit_bytes=62 * 2**20
        ),
    )(
        queries,
        out_grad,
        latents.T,
        norm_gain.reshape(1, width),
        hidden_rows,
        stream_grad,
        latent_proj.T,
        ids.T,
        route.T,
        acts,
        proj,
    )


def settle_kernel(*refs):
    count = (len(refs) - 2) // 3
    arrays, results, held = refs[:count], refs[count : 2 * count], refs[2 * count : 3 * count]
    in_sem, out_sem = refs[-2:]
    loads = [pltpu.make_async_copy(arrays[n], held[n], in_sem.at[n]) for n in range(count)]
    stores = [pltpu.make_async_copy(held[n], results[n], out_sem.at[n]) for n in range(count)]
    for n in range(count):
        loads[n].start()
    for n in range(count):
        loads[n].wait()
        stores[n].start()
    for n in range(count):
        stores[n].wait()


def settle(*arrays):
    hbm = pl.BlockSpec(memory_space=pl.ANY)
    sems = [pltpu.SemaphoreType.DMA((len(arrays),))] * 2
    return pl.pallas_call(
        settle_kernel,
        out_shape=tuple(jax.ShapeDtypeStruct(a.shape, a.dtype) for a in arrays),
        in_specs=[hbm] * len(arrays),
        out_specs=(hbm,) * len(arrays),
        scratch_shapes=[pltpu.VMEM(a.shape, a.dtype) for a in arrays] + sems,
    )(*arrays)


def body(
    queries,
    latents,
    out_grad,
    hidden_rows,
    norm_gain,
    latent_proj,
    stream_grad,
    expert_ids,
    route_weights,
    expert_acts,
    down_proj,
):
    stream_total, act_grad, down_share, weight_grad, query_grad = layer(
        queries,
        latents,
        out_grad,
        hidden_rows,
        norm_gain,
        latent_proj,
        stream_grad,
        expert_ids,
        route_weights,
        expert_acts[0],
        down_proj[0],
    )
    stream_total, act_grad, down_share = settle(stream_total, act_grad, down_share)
    return (query_grad, stream_total, act_grad[None], down_share[None], weight_grad.T)


def solution(mesh):
    in_specs = (
        P("ctx", "exp"),
        P("ctx", None),
        P("ctx", "exp"),
        P(("ctx", "exp"), None),
        P(),
        P(),
        P(("ctx", "exp"), None),
        P(("ctx", "exp"), None),
        P(("ctx", "exp"), None),
        P("exp", "ctx", None),
        P("exp", None, None),
    )
    out_specs = (
        P("ctx", "exp"),
        P(("ctx", "exp"), None),
        P("exp", "ctx", None),
        P("exp", "ctx", None),
        P(("ctx", "exp"), None),
    )
    return jax.shard_map(body, mesh=mesh, in_specs=in_specs, out_specs=out_specs, check_vma=False)
```
